128 devices in a mesh: mem: 8 (over y, x_lo), grid: 16 (over z, x_hi, core).
Axes of the slice: x: 4 (x_hi: 2, x_lo: 2; x = x_hi * 2 + x_lo), y: 4, z: 4, core: 2. Of those that a mesh axis runs over, the one named last changes fastest.
Arguments:
- gradient: float32 [16, 256, 512], P('mem', 'grid'), may hold values from -6 to 6
- members: bfloat16 [128, 16, 256, 512], P('mem', None, 'grid'), may hold values from -6 to 6
- eof_basis: float32 [16, 16], replicated, may hold values from -1.5 to 1.5
- spectral_weight: float32 [16, 128, 256], P(None, None, 'grid'), may hold values from 0.5 to 4
- retained: int32 [16], replicated, may hold values from 32 to 255
- mode_count: int32 [1], replicated, may hold values from 8 to 16
Outputs:
- increment: float32 [16, 256, 512], P('mem', 'grid')
- control: float32 [128, 16, 128, 256], P('mem', None, None, 'grid')
The draws below stay inside these ranges and needn't reach their ends.
All inputs are finite; a program needn't handle non-finite values.
Results may differ from the reference program's by a relative error of at most 0.0003.
Values may be sent and summed in bfloat16 or wider, within the bound.
No kernel may reach another device: no remote copies, remote signals or barrier semaphores. Data moves between devices by JAX's collectives and lax.ppermute only.
A program may use at most 192 MiB of HBM per device.

```python
import math
import jax
import jax.numpy as jnp
from jax import lax

NX = 512
NY = 256
NZ = 16
K = 16
KX = 256
KY = 128
MEMBERS = 128


def set_ends(values, stream_key, smallest, high):
    extent = values.shape
    spot = [jax.random.randint(jax.random.fold_in(stream_key, axis), (), 0, extent[axis]) for axis in range(len(extent))]
    values = values.at[tuple(spot)].set(smallest)
    longest = extent.index(max(extent))
    spot[longest] = (spot[longest] + 1) % extent[longest]
    return values.at[tuple(spot)].set(high)


def shard_levels(stream_key, shape, split, low, largest):
    level = 1.0
    for dim, parts in split:
        steps = jax.random.uniform(jax.random.fold_in(jax.random.fold_in(stream_key, 6), dim), (parts,), jnp.float32, low / len(split), largest / len(split))
        level = level * jnp.repeat(jnp.exp(steps), shape[dim] // parts).reshape((-1,) + (1,) * (len(shape) - 1 - dim))
    return level


def normal_values(rng, dims, deviation, limit, cuts=(), kind=jnp.bfloat16):
    result = jax.random.normal(rng, dims, jnp.float32) * deviation
    if len(cuts) > 0:
        result = shard_levels(rng, dims, cuts, -0.22, 0.18) * result
    return jnp.clip(result, min=-limit, max=limit).astype(kind)


def setup_inputs(seed: int = 0) -> dict:
    key_list = jax.random.split(jax.random.key(seed), 7)
    gradient = normal_values(key_list[0], (NZ, NY, NX), 1.0, 6.0, ((0, 8), (1, 16)), jnp.float32)
    members = normal_values(key_list[1], (MEMBERS, NZ, NY, NX), 1.0, 6.0, ((0, 8), (2, 16)))
    eof_basis = normal_values(key_list[2], (NZ, K), NZ ** -0.5, 1.5, (), jnp.float32)
    spectral_weight = jnp.clip(jnp.exp(math.log(4.0) - 2.0794415 * jax.random.uniform(key_list[3], (K, KY, KX), jnp.float32) ** shard_levels(key_list[3], (K, KY, KX), ((2, 16),), -0.2, 0.2)), 0.5, 4.0)
    retained = set_ends(jax.random.randint(key_list[4], (K,), KY // 4, KY + KX // 2), jax.random.fold_in(key_list[4], 1), KY // 4, (KY + KX // 2) - 1).astype(jnp.int32)
    mode_count = jax.random.randint(key_list[5], (1,), K // 2, K + 1).astype(jnp.int32)
    return {"gradient": gradient, "members": members, "eof_basis": eof_basis, "spectral_weight": spectral_weight, "retained": retained, "mode_count": mode_count}


def cosine_table(length, retain_count):
    cells = jnp.arange(length, dtype=jnp.float32)
    waves = jnp.arange(retain_count, dtype=jnp.float32)
    factor = jnp.where(waves == 0.0, math.sqrt(1.0 / length), math.sqrt(2.0 / length))
    return jnp.cos(math.pi * (cells[:, None] + 0.5) * waves[None, :] / length) * factor[None, :]

def band_filter(weight, retained, offset):
    y_wave = jnp.arange(weight.shape[1], dtype=jnp.int32)[:, None]
    x_wave = offset + jnp.arange(weight.shape[2], dtype=jnp.int32)[None, :]
    inside = (y_wave + x_wave)[None, :, :] < retained[:, None, None]
    return weight * inside.astype(jnp.float32)

def reference(gradient, members, eof_basis, spectral_weight, retained, mode_count):
    high = lax.Precision.HIGHEST
    x_table = cosine_table(NX, KX)
    y_table = cosine_table(NY, KY)
    basis = eof_basis * (jnp.arange(K) < mode_count[0]).astype(jnp.float32)[None, :]
    spectral_filter = band_filter(spectral_weight, retained, 0)
    member_scale = 1.0 / math.sqrt(MEMBERS - 1)

    def one_member(carry, field):
        values = field.astype(jnp.float32)
        product = values * gradient
        projected = jnp.einsum('zk,zyx->kyx', basis, product, precision=high)
        x_spectrum = jnp.einsum('kyx,xp->kyp', projected, x_table, precision=high)
        control = jnp.einsum('yq,kyp->kqp', y_table, x_spectrum, precision=high) * spectral_filter * member_scale
        y_back = jnp.einsum('yq,kqp->kyp', y_table, control * spectral_filter, precision=high)
        x_back = jnp.einsum('kyp,xp->kyx', y_back, x_table, precision=high)
        vertical = jnp.einsum('zk,kyx->zyx', basis, x_back, precision=high)
        return (carry + values * vertical * member_scale, control)
    start = jnp.zeros((NZ, NY, NX), jnp.float32)
    increment, control = lax.scan(one_member, start, members)
    return (increment, control)
```

```python
import functools
import math

import jax
import jax.numpy as jnp
import numpy as np
from jax import lax
from jax.experimental import pallas as pl
from jax.experimental.pallas import tpu as pltpu
from jax.sharding import PartitionSpec as P

F32 = jnp.float32
BF16 = jnp.bfloat16
LANES = 128
CHUNKS = 1
VMEM_LIMIT = 48 * 1024 * 1024


def cosine_table(length, retain_count):
    cells = np.arange(length, dtype=np.float64)
    waves = np.arange(retain_count, dtype=np.float64)
    factor = np.where(waves == 0.0, math.sqrt(1.0 / length), math.sqrt(2.0 / length))
    return np.cos(math.pi * (cells[:, None] + 0.5) * waves[None, :] / length) * factor[None, :]


def table_parts(table):
    high = table.astype(jnp.bfloat16)
    low = (table - high.astype(np.float64)).astype(jnp.bfloat16)
    return high, low


def parts(value):
    high = value.astype(BF16)
    return high, (value - high.astype(F32)).astype(BF16)


def dot3(a, b, dims):
    dot = functools.partial(
        lax.dot_general, dimension_numbers=(dims, ((), ())), preferred_element_type=F32
    )
    return dot(a[0], b[0]) + (dot(a[0], b[1]) + dot(a[1], b[0]))


def regroup(pieces, width):
    pieces = list(pieces)
    count = len(pieces)
    group = lax.broadcasted_iota(jnp.int32, pieces[0].shape, 1) // width
    step = 1
    while step < count:
        upper = (group & step) != 0
        for a in range(count):
            if a & step:
                continue
            low, high = pieces[a], pieces[a | step]
            pieces[a] = jnp.where(upper, pltpu.roll(high, step * width, 1), low)
            pieces[a | step] = jnp.where(
                upper, high, pltpu.roll(low, LANES - step * width, 1)
            )
        step *= 2
    return pieces


def encode(tile):
    peak = jnp.maximum(jnp.max(jnp.abs(tile), axis=0, keepdims=True), 2.0**-80)
    power = jnp.ceil(jnp.log2(peak)) - 15.0
    code = jnp.clip(jnp.round(tile * jnp.exp2(-power)), -32767.0, 32767.0)
    return code.astype(jnp.int32).astype(jnp.int16), power


def spread(basis, rows, transposed):
    count = basis.shape[0]
    size = count * rows
    one = (
        lax.broadcasted_iota(jnp.int32, (size, count), 0) // rows
        == lax.broadcasted_iota(jnp.int32, (size, count), 1)
    ).astype(BF16)
    same = (
        lax.broadcasted_iota(jnp.int32, (size, size), 0) % rows
        == lax.broadcasted_iota(jnp.int32, (size, size), 1) % rows
    )
    out = []
    for part in parts(basis):
        inner = (((1,), (1 if transposed else 0,)), ((), ()))
        left = lax.dot_general(one, part, inner, preferred_element_type=F32).astype(BF16)
        whole = lax.dot_general(
            left, one, (((1,), (1,)), ((), ())), preferred_element_type=F32
        )
        out.append(jnp.where(same, whole, 0.0).astype(BF16))
    return out


def masked_basis(basis_ref, mode_count_ref):
    basis = basis_ref[...]
    mode = lax.broadcasted_iota(jnp.int32, basis.shape, 1)
    return jnp.where(mode < mode_count_ref[0], basis, 0.0)


def tail_tiles(count):
    return -(-2 * count // 16)


def store_powers(power_ref, message_ref, count):
    tiles = tail_tiles(count)
    for j in range(16):
        for t in range(tiles):
            message_ref[j, 2 * count + t] = (
                power_ref[j, 16 * t : 16 * t + 16, :].astype(jnp.int32).astype(jnp.int16)
            )


def load_scales(message_ref, scale_ref, count):
    tiles = tail_tiles(count)
    for j in range(16):
        for t in range(tiles):
            power = message_ref[j, 2 * count + t].astype(jnp.int32).astype(F32)
            scale_ref[j, 16 * t : 16 * t + 16, :] = jnp.exp2(power)


def forward_rows(
    count, mode_count_ref, members_ref, grad_ref, basis_ref, xhi_ref, xlo_ref,
    message_ref, bhi_ref, blo_ref, power_ref,
):
    step = pl.program_id(0)

    @pl.when(step == 0)
    def _():
        hi, lo = spread(masked_basis(basis_ref, mode_count_ref), 16, True)
        bhi_ref[...] = hi
        blo_ref[...] = lo
        power_ref[...] = jnp.zeros_like(power_ref)

    product = (members_ref[0].astype(F32) * grad_ref[...]).reshape(256, 512)
    spectrum = dot3(parts(product), (xhi_ref[...], xlo_ref[...]), ((1,), (0,)))
    modes = dot3((bhi_ref[...], blo_ref[...]), parts(spectrum), ((1,), (0,)))
    for kh in range(2):
        for jh in range(2):
            pieces = [
                modes[(kh * 8 + k) * 16 : (kh * 8 + k + 1) * 16, jh * LANES : (jh + 1) * LANES]
                for k in range(8)
            ]
            for j, piece in enumerate(regroup(pieces, 16)):
                code, power = encode(piece)
                message_ref[jh * 8 + j, 2 * step + kh] = code
                power_ref[jh * 8 + j, pl.ds(2 * step + kh, 1), :] = power

    @pl.when(step == count - 1)
    def _():
        store_powers(power_ref, message_ref, count)


def spectral(
    count, member_scale, retained_ref, offset_ref, message_ref, weight_ref, yhi_ref, ylo_ref,
    control_ref, back_ref, filter_ref, scale_ref, power_ref,
):
    step = pl.program_id(0)

    @pl.when(step == 0)
    def _():
        load_scales(message_ref, scale_ref, count)
        power_ref[...] = jnp.zeros_like(power_ref)
        wave = (
            lax.broadcasted_iota(jnp.int32, (16, LANES), 0)
            + lax.broadcasted_iota(jnp.int32, (16, LANES), 1)
            + offset_ref[0]
        )
        for k in range(16):
            filter_ref[16 * k : 16 * k + 16, :] = jnp.where(
                wave < retained_ref[k], weight_ref[k], 0.0
            )

    y_table = (yhi_ref[...], ylo_ref[...])
    for kh in range(2):
        rows = slice(kh * 128, kh * 128 + 128)
        code = message_ref[:, 2 * step + kh].astype(jnp.int32).astype(F32)
        scale = scale_ref[:, pl.ds(2 * step + kh, 1), :]
        lines = (code * scale).reshape(256, LANES)
        band = filter_ref[rows, :]
        control = dot3(parts(lines), y_table, ((0,), (0,))) * (band * member_scale)
        control_ref[0, kh * 8 : kh * 8 + 8] = control.reshape(8, 16, LANES)
        back = dot3(y_table, parts(control * band), ((1,), (1,)))
        for i in range(16):
            code, power = encode(back[16 * i : 16 * i + 16, :])
            back_ref[i, 2 * step + kh] = code
            power_ref[i, pl.ds(2 * step + kh, 1), :] = power

    @pl.when(step == count - 1)
    def _():
        store_powers(power_ref, back_ref, count)


def backward_rows(
    count, member_scale, first, mode_count_ref, members_ref, back_ref, basis_ref, xhi_ref, xlo_ref,
    *rest,
):
    if first:
        total_ref, bhi_ref, blo_ref, scale_ref, rows_ref = rest
    else:
        before_ref, total_ref, bhi_ref, blo_ref, scale_ref, rows_ref = rest
    step = pl.program_id(0)

    @pl.when(step == 0)
    def _():
        hi, lo = spread(masked_basis(basis_ref, mode_count_ref) * member_scale, 16, False)
        bhi_ref[...] = hi
        blo_ref[...] = lo
        load_scales(back_ref, scale_ref, count)
        if first:
            total_ref[...] = jnp.zeros_like(total_ref)
        else:
            total_ref[...] = before_ref[...]

    for kh in range(2):
        for jh in range(2):
            pieces = []
            for j in range(8):
                code = back_ref[jh * 8 + j, 2 * step + kh].astype(jnp.int32).astype(F32)
                pieces.append(code * scale_ref[jh * 8 + j, pl.ds(2 * step + kh, 1), :])
            for k, piece in enumerate(regroup(pieces, 16)):
                row = (kh * 8 + k) * 16
                rows_ref[row : row + 16, jh * LANES : (jh + 1) * LANES] = piece
    levels = dot3((bhi_ref[...], blo_ref[...]), parts(rows_ref[...]), ((1,), (0,)))
    vertical = dot3(parts(levels), (xhi_ref[...], xlo_ref[...]), ((1,), (1,)))
    total_ref[...] += members_ref[0].astype(F32) * vertical.reshape(16, 16, 512)


def whole(shape):
    return pl.BlockSpec(shape, lambda m: (0,) * len(shape))


SMEM = pl.BlockSpec(memory_space=pltpu.SMEM)


def params():
    return pltpu.CompilerParams(
        dimension_semantics=("arbitrary",), vmem_limit_bytes=VMEM_LIMIT
    )


def local(gradient, members, eof_basis, spectral_weight, retained, mode_count):
    group_count = lax.axis_size("mem")
    held = members.shape[0]
    member_total = held * group_count
    member_scale = 1.0 / math.sqrt(member_total - 1)
    xhi, xlo = (jnp.asarray(t) for t in table_parts(cosine_table(512, 256)))
    yhi, ylo = (jnp.asarray(t) for t in table_parts(cosine_table(256, 128)))
    share = gradient.shape[0]
    spreads = jnp.broadcast_to(gradient[None], (group_count,) + gradient.shape)
    levels = lax.all_to_all(spreads, "mem", 0, 0, tiled=True).reshape(16, 16, 512)
    offset = (lax.axis_index("grid") * 16).astype(jnp.int32).reshape(1)
    weight = spectral_weight.transpose(0, 2, 1)

    count = held // CHUNKS
    tiles = 2 * count + tail_tiles(count)
    tail = 16 * tail_tiles(count)
    message_shape = (16, tiles, 16, LANES)
    message_type = jax.ShapeDtypeStruct(message_shape, jnp.int16)
    basis_scratch = pltpu.VMEM((256, 256), BF16)
    power_scratch = pltpu.VMEM((16, tail, LANES), F32)

    def member_block(chunk):
        return pl.BlockSpec((1, 16, 16, 512), lambda m: (m + chunk * count, 0, 0, 0))

    controls = []
    total = None
    messages = []
    for chunk in range(CHUNKS):
        message = pl.pallas_call(
            functools.partial(forward_rows, count),
            grid=(count,),
            in_specs=[
                SMEM, member_block(chunk), whole((16, 16, 512)), whole((16, 16)),
                whole((512, 256)), whole((512, 256)),
            ],
            out_specs=whole(message_shape),
            out_shape=message_type,
            scratch_shapes=[basis_scratch, basis_scratch, power_scratch],
            compiler_params=params(),
            name="forward_rows",
        )(mode_count, members, levels, eof_basis, xhi, xlo)
        messages.append(lax.all_to_all(message, "grid", 0, 0, tiled=True))
    backs = []
    for chunk in range(CHUNKS):
        control, back = pl.pallas_call(
            functools.partial(spectral, count, member_scale),
            grid=(count,),
            in_specs=[
                SMEM, SMEM, whole(message_shape), whole((16, 16, 128)),
                whole((256, 128)), whole((256, 128)),
            ],
            out_specs=[
                pl.BlockSpec((1, 16, 16, 128), lambda m: (m, 0, 0, 0)), whole(message_shape)
            ],
            out_shape=[jax.ShapeDtypeStruct((count, 16, 16, 128), F32), message_type],
            scratch_shapes=[pltpu.VMEM((256, 128), F32), power_scratch, power_scratch],
            compiler_params=params(),
            name="spectral",
        )(retained, offset, messages[chunk], weight, yhi, ylo)
        controls.append(control)
        backs.append(lax.all_to_all(back, "grid", 0, 0, tiled=True))
    for chunk in range(CHUNKS):
        first = chunk == 0
        total = pl.pallas_call(
            functools.partial(backward_rows, count, member_scale, first),
            grid=(count,),
            in_specs=[
                SMEM, member_block(chunk), whole(message_shape), whole((16, 16)),
                whole((512, 256)), whole((512, 256)),
            ]
            + ([] if first else [whole((16, 16, 512))]),
            out_specs=whole((16, 16, 512)),
            out_shape=jax.ShapeDtypeStruct((16, 16, 512), F32),
            scratch_shapes=[
                basis_scratch, basis_scratch, power_scratch, pltpu.VMEM((256, 256), F32)
            ],
            compiler_params=params(),
            name="backward_rows",
        )(mode_count, members, backs[chunk], eof_basis, xhi, xlo, *([] if first else [total]))
    blocks = total.reshape(group_count, share, 16, 512)
    increment = jnp.sum(lax.all_to_all(blocks, "mem", 0, 0, tiled=True), axis=0)
    control = controls[0] if CHUNKS == 1 else jnp.concatenate(controls, 0)
    return (increment, control.transpose(0, 1, 3, 2))


def solution(mesh):
    return jax.shard_map(
        local,
        mesh=mesh,
        in_specs=(
            P("mem", "grid", None),
            P("mem", None, "grid", None),
            P(),
            P(None, None, "grid"),
            P(),
            P(),
        ),
        out_specs=(P("mem", "grid", None), P("mem", None, None, "grid")),
        check_vma=False,
    )
```

```python
import functools
import math

import jax
import jax.numpy as jnp
import numpy as np
from jax import lax
from jax.experimental import pallas as pl
from jax.experimental.pallas import tpu as pltpu
from jax.sharding import PartitionSpec as P

F32 = jnp.float32
BF16 = jnp.bfloat16
LANES = 128
CHUNKS = 1
GROUP = 4
VMEM_LIMIT = 48 * 1024 * 1024


def cosine_table(length, retain_count):
    cells = np.arange(length, dtype=np.float64)
    waves = np.arange(retain_count, dtype=np.float64)
    factor = np.where(waves == 0.0, math.sqrt(1.0 / length), math.sqrt(2.0 / length))
    return np.cos(math.pi * (cells[:, None] + 0.5) * waves[None, :] / length) * factor[None, :]


def table_parts(table):
    high = table.astype(jnp.bfloat16)
    low = (table - high.astype(np.float64)).astype(jnp.bfloat16)
    return high, low


def parts(value):
    high = value.astype(BF16)
    return high, (value - high.astype(F32)).astype(BF16)


def dot(a, b):
    return lax.dot_general(a, b, (((1,), (0,)), ((), ())), preferred_element_type=F32)


def left_parts(value):
    high, low = parts(value)
    return jnp.concatenate([high, low, high], axis=1)


def right_parts(value):
    high, low = parts(value)
    return jnp.concatenate([high, high, low], axis=0)


def regroup(pieces, width):
    pieces = list(pieces)
    count = len(pieces)
    group = lax.broadcasted_iota(jnp.int32, pieces[0].shape, 1) // width
    step = 1
    while step < count:
        upper = (group & step) != 0
        for a in range(count):
            if a & step:
                continue
            low, high = pieces[a], pieces[a | step]
            pieces[a] = jnp.where(upper, pltpu.roll(high, step * width, 1), low)
            pieces[a | step] = jnp.where(
                upper, high, pltpu.roll(low, LANES - step * width, 1)
            )
        step *= 2
    return pieces


def peak(tile):
    return jnp.max(jnp.abs(tile), axis=0, keepdims=True)


def power_of(peaks):
    return jnp.ceil(jnp.log2(jnp.maximum(peaks, 2.0**-80) * (1.0 + 2.0**-12))) - 15.0


def to_code(scaled):
    return jnp.round(scaled).astype(jnp.int32).astype(jnp.int16)


def from_code(code):
    return code.astype(jnp.int32).astype(F32)


def pick(size, count):
    row = lax.broadcasted_iota(jnp.int32, (size, count), 0) // 16
    return (row == lax.broadcasted_iota(jnp.int32, (size, count), 1)).astype(BF16)


def spread(basis, rows, columns):
    same = (
        lax.broadcasted_iota(jnp.int32, (rows, columns), 0) % 16
        == lax.broadcasted_iota(jnp.int32, (rows, columns), 1) % 16
    )
    out = []
    for part in parts(basis):
        left = dot(pick(rows, 16), part).astype(BF16)
        full = lax.dot_general(
            left, pick(columns, 16), (((1,), (1,)), ((), ())), preferred_element_type=F32
        )
        out.append(jnp.where(same, full, 0.0).astype(BF16))
    return jnp.concatenate([out[0], out[1], out[0]], axis=1)


def masked_basis(basis_ref, mode_count_ref, mode_axis):
    basis = basis_ref[...]
    mode = lax.broadcasted_iota(jnp.int32, basis.shape, mode_axis)
    return jnp.where(mode < mode_count_ref[0], basis, 0.0)


def store_powers(power_ref, message_ref, first_tile):
    groups = power_ref.shape[1]
    for j in range(16):
        for t in range(groups // 2):
            pair = [power_ref[j, 2 * t], power_ref[j, 2 * t + 1]]
            message_ref[j, first_tile + t] = to_code(jnp.concatenate(pair, axis=0))


def forward_rows(
    tiles, modes, mode_count_ref, members_ref, grad_ref, basis_ref, table_ref,
    message_ref, spread_ref, power_ref,
):
    step = pl.program_id(0)
    steps = pl.num_programs(0)

    @pl.when(step == 0)
    def _():
        spread_ref[...] = spread(masked_basis(basis_ref, mode_count_ref, 0), modes * 16, 256)
        power_ref[...] = jnp.zeros_like(power_ref)

    product = members_ref[...].astype(F32) * grad_ref[...][None]
    spectrum = dot(left_parts(product.reshape(GROUP * 256, 512)), table_ref[...])
    combos = []
    for m in range(GROUP):
        out = dot(spread_ref[...], right_parts(spectrum[m * 256 : m * 256 + 256]))
        combos += [out[k * 16 : k * 16 + 16] for k in range(modes)]
    for jh in range(2):
        pieces = [c[:, jh * LANES : (jh + 1) * LANES] for c in combos]
        powers = [
            power_of(jnp.concatenate([peak(pieces[8 * t + c]) for t in range(tiles)], axis=0))
            for c in range(8)
        ]
        shrink = [jnp.exp2(-p) for p in powers]
        for t in range(tiles):
            codes = [to_code(pieces[8 * t + c] * shrink[c][t : t + 1]) for c in range(8)]
            for j, code in enumerate(regroup(codes, 16)):
                message_ref[jh * 8 + j, step * tiles + t] = code
        for j, power in enumerate(regroup(powers, 16)):
            power_ref[jh * 8 + j, step, 0:tiles, :] = power

    @pl.when(step == steps - 1)
    def _():
        store_powers(power_ref, message_ref, message_ref.shape[1] - power_ref.shape[1] // 2)


def spectral(
    tiles, modes, member_scale, retained_ref, offset_ref, message_ref, weight_ref, back_table_ref,
    table_ref, *rest,
):
    control_ref, back_ref, band_ref, scale_ref, power_ref = rest[-5:]
    step = pl.program_id(0)
    steps = pl.num_programs(0)
    groups = power_ref.shape[1]
    first_tail = message_ref.shape[1] - groups // 2

    @pl.when(step == 0)
    def _():
        for i in range(16):
            for t in range(groups // 2):
                scale = jnp.exp2(from_code(message_ref[i, first_tail + t]))
                scale_ref[i, 2 * t] = scale[0:8]
                scale_ref[i, 2 * t + 1] = scale[8:16]
        power_ref[...] = jnp.zeros_like(power_ref)
        wave = (
            lax.broadcasted_iota(jnp.int32, (16, LANES), 0)
            + lax.broadcasted_iota(jnp.int32, (16, LANES), 1)
            + offset_ref[0]
        )
        bands = [jnp.where(wave < retained_ref[k], weight_ref[k], 0.0) for k in range(modes)]
        for t in range(tiles):
            tile = jnp.concatenate([bands[(8 * t + c) % modes] for c in range(8)], axis=0)
            band_ref[:, t * LANES : (t + 1) * LANES] = tile.T

    if modes < 16:
        control_ref[:, modes:] = jnp.zeros((GROUP, 16 - modes, 16, LANES), F32)
    lines = []
    for t in range(tiles):
        code = from_code(message_ref[:, step * tiles + t])
        lines.append((code * scale_ref[:, step, t : t + 1, :]).reshape(256, LANES))
    band = band_ref[...]
    control = dot(table_ref[...], right_parts(jnp.concatenate(lines, axis=1)))
    control = control * (band * member_scale)
    back = dot(back_table_ref[...], right_parts(control * band))
    for t in range(tiles):
        turned = control[:, t * LANES : (t + 1) * LANES].T
        for c in range(8):
            m, k = divmod(8 * t + c, modes)
            control_ref[m, k] = turned[16 * c : 16 * c + 16]
    for i in range(16):
        pieces = [
            back[16 * i : 16 * i + 16, t * LANES : (t + 1) * LANES] for t in range(tiles)
        ]
        power = power_of(jnp.concatenate([peak(p) for p in pieces], axis=0))
        shrink = jnp.exp2(-power)
        for t in range(tiles):
            back_ref[i, step * tiles + t] = to_code(pieces[t] * shrink[t : t + 1])
        power_ref[i, step, 0:tiles, :] = power

    @pl.when(step == steps - 1)
    def _():
        store_powers(power_ref, back_ref, first_tail)


def backward_rows(
    tiles, modes, member_scale, first, mode_count_ref, members_ref, back_ref, basis_ref, table_ref,
    *rest,
):
    if first:
        total_ref, spread_ref, scale_ref = rest
    else:
        before_ref, total_ref, spread_ref, scale_ref = rest
    step = pl.program_id(0)
    groups = scale_ref.shape[2]
    first_tail = back_ref.shape[1] - groups // 2

    @pl.when(step == 0)
    def _():
        basis = masked_basis(basis_ref, mode_count_ref, 1) * member_scale
        spread_ref[...] = spread(basis, 256, modes * 16)
        for jh in range(2):
            for t in range(groups // 2):
                scales = regroup(
                    [jnp.exp2(from_code(back_ref[jh * 8 + j, first_tail + t])) for j in range(8)],
                    16,
                )
                for c in range(8):
                    scale_ref[jh, c, 2 * t] = scales[c][0:8]
                    scale_ref[jh, c, 2 * t + 1] = scales[c][8:16]
        if first:
            total_ref[...] = jnp.zeros_like(total_ref)
        else:
            total_ref[...] = before_ref[...]

    halves = []
    for jh in range(2):
        combos = []
        scales = [scale_ref[jh, c, step] for c in range(8)]
        for t in range(tiles):
            codes = [back_ref[jh * 8 + j, step * tiles + t] for j in range(8)]
            for c, code in enumerate(regroup(codes, 16)):
                combos.append(from_code(code) * scales[c][t : t + 1])
        halves.append(combos)
    levels = []
    for m in range(GROUP):
        rows = [
            jnp.concatenate(half[m * modes : (m + 1) * modes], axis=0) for half in halves
        ]
        levels.append(dot(spread_ref[...], right_parts(jnp.concatenate(rows, axis=1))))
    vertical = dot(left_parts(jnp.concatenate(levels, axis=0)), table_ref[...])
    values = members_ref[...].astype(F32) * vertical.reshape(GROUP, 16, 16, 512)
    total_ref[...] += jnp.sum(values, axis=0)


def whole(shape):
    return pl.BlockSpec(shape, lambda m: (0,) * len(shape))


SMEM = pl.BlockSpec(memory_space=pltpu.SMEM)


def call(kernel, name, steps, operands, in_specs, out_specs, out_shape, scratch, flops, **more):
    return pl.pallas_call(
        kernel,
        grid=(steps,),
        in_specs=in_specs,
        out_specs=out_specs,
        out_shape=out_shape,
        scratch_shapes=scratch,
        compiler_params=pltpu.CompilerParams(
            dimension_semantics=("arbitrary",), vmem_limit_bytes=VMEM_LIMIT
        ),
        cost_estimate=pl.CostEstimate(
            flops=steps * flops, bytes_accessed=steps * flops // 100, transcendentals=0
        ),
        name=name,
        **more,
    )(*operands)


def stacked(table, axis, order):
    both = table_parts(table)
    return jnp.asarray(np.concatenate([both[i] for i in order], axis=axis))


def tables():
    x_table, y_table = cosine_table(512, 256), cosine_table(256, 128)
    return (
        stacked(x_table, 0, (0, 0, 1)),
        stacked(y_table.T, 1, (0, 1, 0)),
        stacked(y_table, 1, (0, 1, 0)),
        stacked(x_table.T, 0, (0, 0, 1)),
    )


def sizes(modes, count):
    groups = count // GROUP
    tiles = modes * GROUP // 8
    padded = groups + groups % 2
    shape = (16, groups * tiles + padded // 2, 16, LANES)
    return groups, tiles, padded, jax.ShapeDtypeStruct(shape, jnp.int16)


def member_block(chunk, groups):
    return pl.BlockSpec((GROUP, 16, 16, 512), lambda m: (m + chunk * groups, 0, 0, 0))


def run_forward(modes, count, chunk, mode_count, members, levels, basis_t, table):
    groups, tiles, padded, message = sizes(modes, count)
    return call(
        functools.partial(forward_rows, tiles, modes), "forward_rows", groups,
        (mode_count, members, levels, basis_t, table),
        [SMEM, member_block(chunk, groups)] + [whole(a.shape) for a in (levels, basis_t, table)],
        whole(message.shape), message,
        [pltpu.VMEM((modes * 16, 768), BF16), pltpu.VMEM((16, padded, 8, LANES), F32)],
        1_600_000_000,
    )


def run_spectral(
    modes, count, chunk, held, member_scale, retained, offset, message, weight, back_table, table,
    control,
):
    groups, tiles, padded, kind = sizes(modes, count)
    extra = [] if control is None else [control]
    return call(
        functools.partial(spectral, tiles, modes, member_scale), "spectral", groups,
        [retained, offset, message, weight, back_table, table] + extra,
        [SMEM, SMEM]
        + [whole(a.shape) for a in (message, weight, back_table, table)]
        + [pl.BlockSpec(memory_space=pl.ANY)] * len(extra),
        [
            pl.BlockSpec((GROUP, 16, 16, LANES), lambda m: (m + chunk * groups, 0, 0, 0)),
            whole(kind.shape),
        ],
        [jax.ShapeDtypeStruct((held, 16, 16, LANES), F32), kind],
        [pltpu.VMEM((LANES, tiles * LANES), F32)]
        + [pltpu.VMEM((16, padded, 8, LANES), F32)] * 2,
        1_000_000_000,
        input_output_aliases={6: 0} if extra else {},
    )


def run_backward(
    modes, count, chunk, member_scale, mode_count, members, back, basis, table, total
):
    groups, tiles, padded, _ = sizes(modes, count)
    extra = [] if total is None else [total]
    return call(
        functools.partial(backward_rows, tiles, modes, member_scale, total is None),
        "backward_rows", groups,
        [mode_count, members, back, basis, table] + extra,
        [SMEM, member_block(chunk, groups)]
        + [whole(a.shape) for a in [back, basis, table] + extra],
        whole((16, 16, 512)), jax.ShapeDtypeStruct((16, 16, 512), F32),
        [
            pltpu.VMEM((256, modes * 48), BF16),
            pltpu.VMEM((2, 8, padded, 8, LANES), F32),
        ],
        1_600_000_000,
    )


def local(gradient, members, eof_basis, spectral_weight, retained, mode_count):
    group_count = lax.axis_size("mem")
    held, share = members.shape[0], gradient.shape[0]
    member_scale = 1.0 / math.sqrt(held * group_count - 1)
    x_forward, y_forward, y_back, x_back = tables()
    copies = jnp.broadcast_to(gradient[None], (group_count,) + gradient.shape)
    levels = lax.all_to_all(copies, "mem", 0, 0, tiled=True).reshape(16, 16, 512)
    offset = (lax.axis_index("grid") * 16).astype(jnp.int32).reshape(1)
    weight = spectral_weight.transpose(0, 2, 1)
    basis_t = eof_basis.T
    modes, count = 16, held // CHUNKS

    messages, backs = [], []
    control = total = None
    for chunk in range(CHUNKS):
        message = run_forward(
            modes, count, chunk, mode_count, members, levels, basis_t, x_forward
        )
        messages.append(lax.all_to_all(message, "grid", 0, 0, tiled=True))
    for chunk in range(CHUNKS):
        control, back = run_spectral(
            modes, count, chunk, held, member_scale, retained, offset, messages[chunk], weight,
            y_back, y_forward, control,
        )
        backs.append(lax.all_to_all(back, "grid", 0, 0, tiled=True))
    for chunk in range(CHUNKS):
        total = run_backward(
            modes, count, chunk, member_scale, mode_count, members, backs[chunk], eof_basis,
            x_back, total,
        )
    blocks = total.reshape(group_count, share, 16, 512)
    increment = jnp.sum(lax.all_to_all(blocks, "mem", 0, 0, tiled=True), axis=0)
    return (increment, control.transpose(0, 1, 3, 2))


def solution(mesh):
    return jax.shard_map(
        local,
        mesh=mesh,
        in_specs=(
            P("mem", "grid", None),
            P("mem", None, "grid", None),
            P(),
            P(None, None, "grid"),
            P(),
            P(),
        ),
        out_specs=(P("mem", "grid", None), P("mem", None, None, "grid")),
        check_vma=False,
    )
```

```python
import functools
import math

import jax
import jax.numpy as jnp
import numpy as np
from jax import lax
from jax.experimental import pallas as pl
from jax.experimental.pallas import tpu as pltpu
from jax.sharding import PartitionSpec as P

F32 = jnp.float32
BF16 = jnp.bfloat16
LANES = 128
CHUNKS = 1
GROUP = 4
MODE_STEPS = (8, 10, 12, 14, 16)
VMEM_LIMIT = 48 * 1024 * 1024


def cosine_table(length, retain_count):
    cells = np.arange(length, dtype=np.float64)
    waves = np.arange(retain_count, dtype=np.float64)
    factor = np.where(waves == 0.0, math.sqrt(1.0 / length), math.sqrt(2.0 / length))
    return np.cos(math.pi * (cells[:, None] + 0.5) * waves[None, :] / length) * factor[None, :]


def table_parts(table):
    high = table.astype(jnp.bfloat16)
    low = (table - high.astype(np.float64)).astype(jnp.bfloat16)
    return high, low


def parts(value):
    high = value.astype(BF16)
    return high, (value - high.astype(F32)).astype(BF16)


def dot(a, b):
    return lax.dot_general(a, b, (((1,), (0,)), ((), ())), preferred_element_type=F32)


def left_parts(value):
    high, low = parts(value)
    return jnp.concatenate([high, low, high], axis=1)


def right_parts(value):
    high, low = parts(value)
    return jnp.concatenate([high, high, low], axis=0)


def regroup(pieces, width):
    pieces = list(pieces)
    count = len(pieces)
    group = lax.broadcasted_iota(jnp.int32, pieces[0].shape, 1) // width
    step = 1
    while step < count:
        upper = (group & step) != 0
        for a in range(count):
            if a & step:
                continue
            low, high = pieces[a], pieces[a | step]
            pieces[a] = jnp.where(upper, pltpu.roll(high, step * width, 1), low)
            pieces[a | step] = jnp.where(
                upper, high, pltpu.roll(low, LANES - step * width, 1)
            )
        step *= 2
    return pieces


def peak(tile):
    return jnp.max(jnp.abs(tile), axis=0, keepdims=True)


def power_of(peaks):
    return jnp.ceil(jnp.log2(jnp.maximum(peaks, 2.0**-80) * (1.0 + 2.0**-12))) - 15.0


def to_code(scaled):
    return jnp.round(scaled).astype(jnp.int32).astype(jnp.int16)


def from_code(code):
    return code.astype(jnp.int32).astype(F32)


def pick(size, count):
    row = lax.broadcasted_iota(jnp.int32, (size, count), 0) // 16
    return (row == lax.broadcasted_iota(jnp.int32, (size, count), 1)).astype(BF16)


def spread(basis, rows, columns):
    same = (
        lax.broadcasted_iota(jnp.int32, (rows, columns), 0) % 16
        == lax.broadcasted_iota(jnp.int32, (rows, columns), 1) % 16
    )
    out = []
    for part in parts(basis):
        left = dot(pick(rows, 16), part).astype(BF16)
        full = lax.dot_general(
            left, pick(columns, 16), (((1,), (1,)), ((), ())), preferred_element_type=F32
        )
        out.append(jnp.where(same, full, 0.0).astype(BF16))
    return jnp.concatenate([out[0], out[1], out[0]], axis=1)


def masked_basis(basis_ref, mode_count_ref, mode_axis):
    basis = basis_ref[...]
    mode = lax.broadcasted_iota(jnp.int32, basis.shape, mode_axis)
    return jnp.where(mode < mode_count_ref[0], basis, 0.0)


def store_powers(power_ref, message_ref, first_tile):
    groups = power_ref.shape[1]
    for j in range(16):
        for t in range(groups // 2):
            pair = [power_ref[j, 2 * t], power_ref[j, 2 * t + 1]]
            message_ref[j, first_tile + t] = to_code(jnp.concatenate(pair, axis=0))


def forward_rows(
    tiles, modes, mode_count_ref, members_ref, grad_ref, basis_ref, table_ref,
    message_ref, spread_ref, power_ref,
):
    step = pl.program_id(0)
    steps = pl.num_programs(0)

    @pl.when(step == 0)
    def _():
        spread_ref[...] = spread(masked_basis(basis_ref, mode_count_ref, 0), modes * 16, 256)
        power_ref[...] = jnp.zeros_like(power_ref)

    product = members_ref[...].astype(F32) * grad_ref[...][None]
    spectrum = dot(left_parts(product.reshape(GROUP * 256, 512)), table_ref[...])
    combos = []
    for m in range(GROUP):
        out = dot(spread_ref[...], right_parts(spectrum[m * 256 : m * 256 + 256]))
        combos += [out[k * 16 : k * 16 + 16] for k in range(modes)]
    for jh in range(2):
        pieces = [c[:, jh * LANES : (jh + 1) * LANES] for c in combos]
        powers = [
            power_of(jnp.concatenate([peak(pieces[8 * t + c]) for t in range(tiles)], axis=0))
            for c in range(8)
        ]
        shrink = [jnp.exp2(-p) for p in powers]
        for t in range(tiles):
            codes = [to_code(pieces[8 * t + c] * shrink[c][t : t + 1]) for c in range(8)]
            for j, code in enumerate(regroup(codes, 16)):
                message_ref[jh * 8 + j, step * tiles + t] = code
        for j, power in enumerate(regroup(powers, 16)):
            power_ref[jh * 8 + j, step, 0:tiles, :] = power

    @pl.when(step == steps - 1)
    def _():
        store_powers(power_ref, message_ref, message_ref.shape[1] - power_ref.shape[1] // 2)


def spectral(
    tiles, modes, member_scale, retained_ref, offset_ref, message_ref, weight_ref, back_table_ref,
    table_ref, *rest,
):
    control_ref, back_ref, band_ref, scale_ref, power_ref = rest[-5:]
    step = pl.program_id(0)
    steps = pl.num_programs(0)
    groups = power_ref.shape[1]
    first_tail = message_ref.shape[1] - groups // 2

    @pl.when(step == 0)
    def _():
        for i in range(16):
            for t in range(groups // 2):
                scale = jnp.exp2(from_code(message_ref[i, first_tail + t]))
                scale_ref[i, 2 * t] = scale[0:8]
                scale_ref[i, 2 * t + 1] = scale[8:16]
        power_ref[...] = jnp.zeros_like(power_ref)
        wave = (
            lax.broadcasted_iota(jnp.int32, (16, LANES), 0)
            + lax.broadcasted_iota(jnp.int32, (16, LANES), 1)
            + offset_ref[0]
        )
        bands = [jnp.where(wave < retained_ref[k], weight_ref[k], 0.0) for k in range(modes)]
        for t in range(tiles):
            tile = jnp.concatenate([bands[(8 * t + c) % modes] for c in range(8)], axis=0)
            band_ref[:, t * LANES : (t + 1) * LANES] = tile.T

    if modes < 16:
        control_ref[:, modes:] = jnp.zeros((GROUP, 16 - modes, 16, LANES), F32)
    lines = []
    for t in range(tiles):
        code = from_code(message_ref[:, step * tiles + t])
        lines.append((code * scale_ref[:, step, t : t + 1, :]).reshape(256, LANES))
    band = band_ref[...]
    control = dot(table_ref[...], right_parts(jnp.concatenate(lines, axis=1)))
    control = control * (band * member_scale)
    back = dot(back_table_ref[...], right_parts(control * band))
    for t in range(tiles):
        turned = control[:, t * LANES : (t + 1) * LANES].T
        for c in range(8):
            m, k = divmod(8 * t + c, modes)
            control_ref[m, k] = turned[16 * c : 16 * c + 16]
    for i in range(16):
        pieces = [
            back[16 * i : 16 * i + 16, t * LANES : (t + 1) * LANES] for t in range(tiles)
        ]
        power = power_of(jnp.concatenate([peak(p) for p in pieces], axis=0))
        shrink = jnp.exp2(-power)
        for t in range(tiles):
            back_ref[i, step * tiles + t] = to_code(pieces[t] * shrink[t : t + 1])
        power_ref[i, step, 0:tiles, :] = power

    @pl.when(step == steps - 1)
    def _():
        store_powers(power_ref, back_ref, first_tail)


def backward_rows(
    tiles, modes, member_scale, first, mode_count_ref, members_ref, back_ref, basis_ref, table_ref,
    *rest,
):
    if first:
        total_ref, spread_ref, scale_ref = rest
    else:
        before_ref, total_ref, spread_ref, scale_ref = rest
    step = pl.program_id(0)
    groups = scale_ref.shape[2]
    first_tail = back_ref.shape[1] - groups // 2

    @pl.when(step == 0)
    def _():
        basis = masked_basis(basis_ref, mode_count_ref, 1) * member_scale
        spread_ref[...] = spread(basis, 256, modes * 16)
        for jh in range(2):
            for t in range(groups // 2):
                scales = regroup(
                    [jnp.exp2(from_code(back_ref[jh * 8 + j, first_tail + t])) for j in range(8)],
                    16,
                )
                for c in range(8):
                    scale_ref[jh, c, 2 * t] = scales[c][0:8]
                    scale_ref[jh, c, 2 * t + 1] = scales[c][8:16]
        if first:
            total_ref[...] = jnp.zeros_like(total_ref)
        else:
            total_ref[...] = before_ref[...]

    halves = []
    for jh in range(2):
        combos = []
        scales = [scale_ref[jh, c, step] for c in range(8)]
        for t in range(tiles):
            codes = [back_ref[jh * 8 + j, step * tiles + t] for j in range(8)]
            for c, code in enumerate(regroup(codes, 16)):
                combos.append(from_code(code) * scales[c][t : t + 1])
        halves.append(combos)
    levels = []
    for m in range(GROUP):
        rows = [
            jnp.concatenate(half[m * modes : (m + 1) * modes], axis=0) for half in halves
        ]
        levels.append(dot(spread_ref[...], right_parts(jnp.concatenate(rows, axis=1))))
    vertical = dot(left_parts(jnp.concatenate(levels, axis=0)), table_ref[...])
    values = members_ref[...].astype(F32) * vertical.reshape(GROUP, 16, 16, 512)
    total_ref[...] += jnp.sum(values, axis=0)


def whole(shape):
    return pl.BlockSpec(shape, lambda m: (0,) * len(shape))


SMEM = pl.BlockSpec(memory_space=pltpu.SMEM)


def call(kernel, name, steps, operands, in_specs, out_specs, out_shape, scratch, flops, **more):
    return pl.pallas_call(
        kernel,
        grid=(steps,),
        in_specs=in_specs,
        out_specs=out_specs,
        out_shape=out_shape,
        scratch_shapes=scratch,
        compiler_params=pltpu.CompilerParams(
            dimension_semantics=("arbitrary",), vmem_limit_bytes=VMEM_LIMIT
        ),
        cost_estimate=pl.CostEstimate(
            flops=steps * flops, bytes_accessed=steps * flops // 100, transcendentals=0
        ),
        name=name,
        **more,
    )(*operands)


def stacked(table, axis, order):
    both = table_parts(table)
    return jnp.asarray(np.concatenate([both[i] for i in order], axis=axis))


def tables():
    x_table, y_table = cosine_table(512, 256), cosine_table(256, 128)
    return (
        stacked(x_table, 0, (0, 0, 1)),
        stacked(y_table.T, 1, (0, 1, 0)),
        stacked(y_table, 1, (0, 1, 0)),
        stacked(x_table.T, 0, (0, 0, 1)),
    )


def sizes(modes, count):
    groups = count // GROUP
    tiles = modes * GROUP // 8
    padded = groups + groups % 2
    shape = (16, groups * tiles + padded // 2, 16, LANES)
    return groups, tiles, padded, jax.ShapeDtypeStruct(shape, jnp.int16)


def member_block(chunk, groups):
    return pl.BlockSpec((GROUP, 16, 16, 512), lambda m: (m + chunk * groups, 0, 0, 0))


def run_forward(modes, count, chunk, mode_count, members, levels, basis_t, table):
    groups, tiles, padded, message = sizes(modes, count)
    return call(
        functools.partial(forward_rows, tiles, modes), "forward_rows", groups,
        (mode_count, members, levels, basis_t, table),
        [SMEM, member_block(chunk, groups)] + [whole(a.shape) for a in (levels, basis_t, table)],
        whole(message.shape), message,
        [pltpu.VMEM((modes * 16, 768), BF16), pltpu.VMEM((16, padded, 8, LANES), F32)],
        1_600_000_000,
    )


def run_spectral(
    modes, count, chunk, held, member_scale, retained, offset, message, weight, back_table, table,
    control,
):
    groups, tiles, padded, kind = sizes(modes, count)
    extra = [] if control is None else [control]
    return call(
        functools.partial(spectral, tiles, modes, member_scale), "spectral", groups,
        [retained, offset, message, weight, back_table, table] + extra,
        [SMEM, SMEM]
        + [whole(a.shape) for a in (message, weight, back_table, table)]
        + [pl.BlockSpec(memory_space=pl.ANY)] * len(extra),
        [
            pl.BlockSpec((GROUP, 16, 16, LANES), lambda m: (m + chunk * groups, 0, 0, 0)),
            whole(kind.shape),
        ],
        [jax.ShapeDtypeStruct((held, 16, 16, LANES), F32), kind],
        [pltpu.VMEM((LANES, tiles * LANES), F32)]
        + [pltpu.VMEM((16, padded, 8, LANES), F32)] * 2,
        1_000_000_000,
        input_output_aliases={6: 0} if extra else {},
    )


def run_backward(
    modes, count, chunk, member_scale, mode_count, members, back, basis, table, total
):
    groups, tiles, padded, _ = sizes(modes, count)
    extra = [] if total is None else [total]
    return call(
        functools.partial(backward_rows, tiles, modes, member_scale, total is None),
        "backward_rows", groups,
        [mode_count, members, back, basis, table] + extra,
        [SMEM, member_block(chunk, groups)]
        + [whole(a.shape) for a in [back, basis, table] + extra],
        whole((16, 16, 512)), jax.ShapeDtypeStruct((16, 16, 512), F32),
        [
            pltpu.VMEM((256, modes * 48), BF16),
            pltpu.VMEM((2, 8, padded, 8, LANES), F32),
        ],
        1_600_000_000,
    )


def local(gradient, members, eof_basis, spectral_weight, retained, mode_count):
    group_count = lax.axis_size("mem")
    held, share = members.shape[0], gradient.shape[0]
    member_scale = 1.0 / math.sqrt(held * group_count - 1)
    x_forward, y_forward, y_back, x_back = tables()
    copies = jnp.broadcast_to(gradient[None], (group_count,) + gradient.shape)
    levels = lax.all_to_all(copies, "mem", 0, 0, tiled=True).reshape(16, 16, 512)
    offset = (lax.axis_index("grid") * 16).astype(jnp.int32).reshape(1)
    weight = spectral_weight.transpose(0, 2, 1)
    basis_t = eof_basis.T
    count = held // CHUNKS

    def chain(modes):
        messages, backs = [], []
        control = total = None
        for chunk in range(CHUNKS):
            message = run_forward(
                modes, count, chunk, mode_count, members, levels, basis_t, x_forward
            )
            messages.append(lax.all_to_all(message, "grid", 0, 0, tiled=True))
        for chunk in range(CHUNKS):
            control, back = run_spectral(
                modes, count, chunk, held, member_scale, retained, offset, messages[chunk],
                weight, y_back, y_forward, control,
            )
            backs.append(lax.all_to_all(back, "grid", 0, 0, tiled=True))
        for chunk in range(CHUNKS):
            total = run_backward(
                modes, count, chunk, member_scale, mode_count, members, backs[chunk], eof_basis,
                x_back, total,
            )
        return total, control

    most = len(MODE_STEPS) - 1
    branch = sum((mode_count[0] > m).astype(jnp.int32) for m in MODE_STEPS[:most])
    total, control = lax.switch(branch, [functools.partial(chain, m) for m in MODE_STEPS])
    blocks = total.reshape(group_count, share, 16, 512)
    increment = jnp.sum(lax.all_to_all(blocks, "mem", 0, 0, tiled=True), axis=0)
    return (increment, control.transpose(0, 1, 3, 2))


def solution(mesh):
    return jax.shard_map(
        local,
        mesh=mesh,
        in_specs=(
            P("mem", "grid", None),
            P("mem", None, "grid", None),
            P(),
            P(None, None, "grid"),
            P(),
            P(),
        ),
        out_specs=(P("mem", "grid", None), P("mem", None, None, "grid")),
        check_vma=False,
    )
```

```python
import functools
import math

import jax
import jax.numpy as jnp
import numpy as np
from jax import lax
from jax.experimental import pallas as pl
from jax.experimental.pallas import tpu as pltpu
from jax.sharding import PartitionSpec as P

F32 = jnp.float32
BF16 = jnp.bfloat16
LANES = 128
GROUP = 4
MODE_STEPS = (8, 10, 12, 14, 16)
VMEM_LIMIT = 48 * 1024 * 1024


def cosine_table(length, retain_count):
    cells = np.arange(length, dtype=np.float64)
    waves = np.arange(retain_count, dtype=np.float64)
    factor = np.where(waves == 0.0, math.sqrt(1.0 / length), math.sqrt(2.0 / length))
    return np.cos(math.pi * (cells[:, None] + 0.5) * waves[None, :] / length) * factor[None, :]


def table_parts(table):
    high = table.astype(jnp.bfloat16)
    low = (table - high.astype(np.float64)).astype(jnp.bfloat16)
    return high, low


def parts(value):
    high = value.astype(BF16)
    return high, (value - high.astype(F32)).astype(BF16)


def dot(a, b):
    return lax.dot_general(a, b, (((1,), (0,)), ((), ())), preferred_element_type=F32)


def left_parts(value):
    high, low = parts(value)
    return jnp.concatenate([high, low, high], axis=1)


def right_parts(value):
    high, low = parts(value)
    return jnp.concatenate([high, high, low], axis=0)


def regroup(pieces, width):
    pieces = list(pieces)
    count = len(pieces)
    group = lax.broadcasted_iota(jnp.int32, pieces[0].shape, 1) // width
    step = 1
    while step < count:
        upper = (group & step) != 0
        for a in range(count):
            if a & step:
                continue
            low, high = pieces[a], pieces[a | step]
            pieces[a] = jnp.where(upper, pltpu.roll(high, step * width, 1), low)
            pieces[a | step] = jnp.where(
                upper, high, pltpu.roll(low, LANES - step * width, 1)
            )
        step *= 2
    return pieces


def peak(tile):
    return jnp.max(jnp.abs(tile), axis=0, keepdims=True)


def power_of(peaks):
    return jnp.ceil(jnp.log2(jnp.maximum(peaks, 2.0**-80) * (1.0 + 2.0**-12))) - 15.0


def to_code(scaled):
    return jnp.round(scaled).astype(jnp.int32).astype(jnp.int16)


def from_code(code):
    return code.astype(jnp.int32).astype(F32)


def pick(size, count):
    row = lax.broadcasted_iota(jnp.int32, (size, count), 0) // 16
    return (row == lax.broadcasted_iota(jnp.int32, (size, count), 1)).astype(BF16)


def spread(basis, rows, columns):
    same = (
        lax.broadcasted_iota(jnp.int32, (rows, columns), 0) % 16
        == lax.broadcasted_iota(jnp.int32, (rows, columns), 1) % 16
    )
    out = []
    for part in parts(basis):
        left = dot(pick(rows, 16), part).astype(BF16)
        full = lax.dot_general(
            left, pick(columns, 16), (((1,), (1,)), ((), ())), preferred_element_type=F32
        )
        out.append(jnp.where(same, full, 0.0).astype(BF16))
    return jnp.concatenate([out[0], out[1], out[0]], axis=1)


def masked_basis(basis_ref, mode_count_ref, mode_axis):
    basis = basis_ref[...]
    mode = lax.broadcasted_iota(jnp.int32, basis.shape, mode_axis)
    return jnp.where(mode < mode_count_ref[0], basis, 0.0)


def store_powers(power_ref, message_ref, first_tile):
    groups = power_ref.shape[1]
    for j in range(16):
        for t in range(groups // 2):
            pair = [power_ref[j, 2 * t], power_ref[j, 2 * t + 1]]
            message_ref[j, first_tile + t] = to_code(jnp.concatenate(pair, axis=0))


def encode_levels(levels):
    tiles = [
        levels[z][:, q * LANES : (q + 1) * LANES] for z in range(levels.shape[0]) for q in range(4)
    ]
    power = power_of(jnp.concatenate([peak(t) for t in tiles], axis=0))
    shrink = jnp.exp2(-power)
    codes = [to_code(t * shrink[n : n + 1]) for n, t in enumerate(tiles)]
    tail = jnp.concatenate([power, jnp.zeros((16 - len(tiles), LANES), F32)], axis=0)
    return codes + [to_code(tail)]


def decode_levels(code_ref, source):
    tiles = code_ref.shape[1] - 1
    scale = jnp.exp2(from_code(code_ref[source, tiles]))
    values = [from_code(code_ref[source, n]) * scale[n : n + 1] for n in range(tiles)]
    return [jnp.concatenate(values[z : z + 4], axis=1) for z in range(0, tiles, 4)]


def encode_gradient(gradient_ref, code_ref):
    for n, code in enumerate(encode_levels(gradient_ref[...])):
        for target in range(code_ref.shape[0]):
            code_ref[target, n] = code


def add_groups(code_ref, increment_ref):
    total = decode_levels(code_ref, 0)
    for source in range(1, code_ref.shape[0]):
        total = [a + b for a, b in zip(total, decode_levels(code_ref, source))]
    for z, level in enumerate(total):
        increment_ref[z] = level


def forward_rows(
    tiles, modes, mode_count_ref, members_ref, code_ref, basis_ref, table_ref,
    message_ref, spread_ref, power_ref, grad_ref,
):
    step = pl.program_id(0)
    steps = pl.num_programs(0)

    @pl.when(step == 0)
    def _():
        spread_ref[...] = spread(masked_basis(basis_ref, mode_count_ref, 0), modes * 16, 256)
        power_ref[...] = jnp.zeros_like(power_ref)
        share = 16 // code_ref.shape[0]
        for source in range(code_ref.shape[0]):
            for z, level in enumerate(decode_levels(code_ref, source)):
                grad_ref[share * source + z] = level

    product = members_ref[...].astype(F32) * grad_ref[...][None]
    both = left_parts(product.reshape(GROUP * 256, 512))
    spectra = [dot(both[m * 256 : m * 256 + 256], table_ref[...]) for m in range(GROUP)]
    combos = []
    for m in range(GROUP):
        out = dot(spread_ref[...], right_parts(spectra[m]))
        combos += [out[k * 16 : k * 16 + 16] for k in range(modes)]
    for jh in range(2):
        pieces = [c[:, jh * LANES : (jh + 1) * LANES] for c in combos]
        powers = [
            power_of(jnp.concatenate([peak(pieces[8 * t + c]) for t in range(tiles)], axis=0))
            for c in range(8)
        ]
        shrink = [jnp.exp2(-p) for p in powers]
        for t in range(tiles):
            codes = [to_code(pieces[8 * t + c] * shrink[c][t : t + 1]) for c in range(8)]
            for j, code in enumerate(regroup(codes, 16)):
                message_ref[jh * 8 + j, step * tiles + t] = code
        for j, power in enumerate(regroup(powers, 16)):
            power_ref[jh * 8 + j, step, 0:tiles, :] = power

    @pl.when(step == steps - 1)
    def _():
        store_powers(power_ref, message_ref, message_ref.shape[1] - power_ref.shape[1] // 2)


def spectral(
    tiles, modes, member_scale, retained_ref, offset_ref, message_ref, weight_ref, back_table_ref,
    table_ref, *rest,
):
    control_ref, back_ref, band_ref, scale_ref, power_ref = rest[-5:]
    step = pl.program_id(0)
    steps = pl.num_programs(0)
    groups = power_ref.shape[1]
    first_tail = message_ref.shape[1] - groups // 2

    @pl.when(step == 0)
    def _():
        for i in range(16):
            for t in range(groups // 2):
                scale = jnp.exp2(from_code(message_ref[i, first_tail + t]))
                scale_ref[i, 2 * t] = scale[0:8]
                scale_ref[i, 2 * t + 1] = scale[8:16]
        power_ref[...] = jnp.zeros_like(power_ref)
        wave = (
            lax.broadcasted_iota(jnp.int32, (16, LANES), 0)
            + lax.broadcasted_iota(jnp.int32, (16, LANES), 1)
            + offset_ref[0]
        )
        bands = [jnp.where(wave < retained_ref[k], weight_ref[k], 0.0) for k in range(modes)]
        for t in range(tiles):
            tile = jnp.concatenate([bands[(8 * t + c) % modes] for c in range(8)], axis=0)
            band_ref[:, t * LANES : (t + 1) * LANES] = tile.T

    if modes < 16:
        control_ref[:, modes:] = jnp.zeros((GROUP, 16 - modes, 16, LANES), F32)
    lines = []
    for t in range(tiles):
        code = from_code(message_ref[:, step * tiles + t])
        lines.append((code * scale_ref[:, step, t : t + 1, :]).reshape(256, LANES))
    band = band_ref[...]
    control = dot(table_ref[...], right_parts(jnp.concatenate(lines, axis=1)))
    control = control * (band * member_scale)
    back = dot(back_table_ref[...], right_parts(control * band))
    for t in range(tiles):
        turned = control[:, t * LANES : (t + 1) * LANES].T
        for c in range(8):
            m, k = divmod(8 * t + c, modes)
            control_ref[m, k] = turned[16 * c : 16 * c + 16]
    for i in range(16):
        pieces = [
            back[16 * i : 16 * i + 16, t * LANES : (t + 1) * LANES] for t in range(tiles)
        ]
        power = power_of(jnp.concatenate([peak(p) for p in pieces], axis=0))
        shrink = jnp.exp2(-power)
        for t in range(tiles):
            back_ref[i, step * tiles + t] = to_code(pieces[t] * shrink[t : t + 1])
        power_ref[i, step, 0:tiles, :] = power

    @pl.when(step == steps - 1)
    def _():
        store_powers(power_ref, back_ref, first_tail)


def backward_rows(
    tiles, modes, member_scale, mode_count_ref, members_ref, back_ref, basis_ref, table_ref,
    *rest,
):
    code_ref, spread_ref, scale_ref, total_ref = rest
    step = pl.program_id(0)
    groups = scale_ref.shape[2]
    first_tail = back_ref.shape[1] - groups // 2

    @pl.when(step == 0)
    def _():
        basis = masked_basis(basis_ref, mode_count_ref, 1) * member_scale
        spread_ref[...] = spread(basis, 256, modes * 16)
        for jh in range(2):
            for t in range(groups // 2):
                scales = regroup(
                    [jnp.exp2(from_code(back_ref[jh * 8 + j, first_tail + t])) for j in range(8)],
                    16,
                )
                for c in range(8):
                    scale_ref[jh, c, 2 * t] = scales[c][0:8]
                    scale_ref[jh, c, 2 * t + 1] = scales[c][8:16]
        total_ref[...] = jnp.zeros_like(total_ref)

    halves = []
    for jh in range(2):
        combos = []
        scales = [scale_ref[jh, c, step] for c in range(8)]
        for t in range(tiles):
            codes = [back_ref[jh * 8 + j, step * tiles + t] for j in range(8)]
            for c, code in enumerate(regroup(codes, 16)):
                combos.append(from_code(code) * scales[c][t : t + 1])
        halves.append(combos)
    levels = []
    for m in range(GROUP):
        rows = [
            jnp.concatenate(half[m * modes : (m + 1) * modes], axis=0) for half in halves
        ]
        levels.append(dot(spread_ref[...], right_parts(jnp.concatenate(rows, axis=1))))
    vertical = dot(left_parts(jnp.concatenate(levels, axis=0)), table_ref[...])
    values = members_ref[...].astype(F32) * vertical.reshape(GROUP, 16, 16, 512)
    total_ref[...] += jnp.sum(values, axis=0)

    @pl.when(step == pl.num_programs(0) - 1)
    def _():
        share = 16 // code_ref.shape[0]
        for target in range(code_ref.shape[0]):
            levels = total_ref[share * target : share * (target + 1)]
            for n, code in enumerate(encode_levels(levels)):
                code_ref[target, n] = code


def whole(shape):
    return pl.BlockSpec(shape, lambda m: (0,) * len(shape))


SMEM = pl.BlockSpec(memory_space=pltpu.SMEM)


def call(kernel, name, steps, operands, in_specs, out_specs, out_shape, scratch, flops, **more):
    return pl.pallas_call(
        kernel,
        grid=(steps,),
        in_specs=in_specs,
        out_specs=out_specs,
        out_shape=out_shape,
        scratch_shapes=scratch,
        compiler_params=pltpu.CompilerParams(
            dimension_semantics=("arbitrary",), vmem_limit_bytes=VMEM_LIMIT
        ),
        cost_estimate=pl.CostEstimate(
            flops=steps * flops, bytes_accessed=steps * flops // 100, transcendentals=0
        ),
        name=name,
        **more,
    )(*operands)


def stacked(table, axis, order):
    both = table_parts(table)
    return jnp.asarray(np.concatenate([both[i] for i in order], axis=axis))


def tables():
    x_table, y_table = cosine_table(512, 256), cosine_table(256, 128)
    return (
        stacked(x_table, 0, (0, 0, 1)),
        stacked(y_table.T, 1, (0, 1, 0)),
        stacked(y_table, 1, (0, 1, 0)),
        stacked(x_table.T, 0, (0, 0, 1)),
    )


def sizes(modes, count):
    groups = count // GROUP
    tiles = modes * GROUP // 8
    padded = groups + groups % 2
    shape = (16, groups * tiles + padded // 2, 16, LANES)
    return groups, tiles, padded, jax.ShapeDtypeStruct(shape, jnp.int16)


def member_block(chunk, groups):
    return pl.BlockSpec((GROUP, 16, 16, 512), lambda m: (m + chunk * groups, 0, 0, 0))


def run_forward(modes, count, chunk, mode_count, members, levels, basis_t, table):
    groups, tiles, padded, message = sizes(modes, count)
    return call(
        functools.partial(forward_rows, tiles, modes), "forward_rows", groups,
        (mode_count, members, levels, basis_t, table),
        [SMEM, member_block(chunk, groups)] + [whole(a.shape) for a in (levels, basis_t, table)],
        whole(message.shape), message,
        [
            pltpu.VMEM((modes * 16, 768), BF16),
            pltpu.VMEM((16, padded, 8, LANES), F32),
            pltpu.VMEM((16, 16, 512), F32),
        ],
        1_600_000_000,
    )


def run_spectral(
    modes, count, chunk, held, member_scale, retained, offset, message, weight, back_table, table,
    control,
):
    groups, tiles, padded, kind = sizes(modes, count)
    extra = [] if control is None else [control]
    return call(
        functools.partial(spectral, tiles, modes, member_scale), "spectral", groups,
        [retained, offset, message, weight, back_table, table] + extra,
        [SMEM, SMEM]
        + [whole(a.shape) for a in (message, weight, back_table, table)]
        + [pl.BlockSpec(memory_space=pl.ANY)] * len(extra),
        [
            pl.BlockSpec((GROUP, 16, 16, LANES), lambda m: (m + chunk * groups, 0, 0, 0)),
            whole(kind.shape),
        ],
        [jax.ShapeDtypeStruct((held, 16, 16, LANES), F32), kind],
        [pltpu.VMEM((LANES, tiles * LANES), F32)]
        + [pltpu.VMEM((16, padded, 8, LANES), F32)] * 2,
        1_000_000_000,
        input_output_aliases={6: 0} if extra else {},
    )


def run_backward(modes, group_count, member_scale, mode_count, members, back, basis, table):
    groups, tiles, padded, _ = sizes(modes, members.shape[0])
    shape = code_shape(group_count)
    return call(
        functools.partial(backward_rows, tiles, modes, member_scale), "backward_rows", groups,
        [mode_count, members, back, basis, table],
        [SMEM, member_block(0, groups)] + [whole(a.shape) for a in [back, basis, table]],
        whole(shape), jax.ShapeDtypeStruct(shape, jnp.int16),
        [
            pltpu.VMEM((256, modes * 48), BF16),
            pltpu.VMEM((2, 8, padded, 8, LANES), F32),
            pltpu.VMEM((16, 16, 512), F32),
        ],
        1_600_000_000,
    )


def code_shape(group_count):
    return (group_count, 64 // group_count + 1, 16, LANES)


def local(gradient, members, eof_basis, spectral_weight, retained, mode_count):
    group_count = lax.axis_size("mem")
    held = members.shape[0]
    member_scale = 1.0 / math.sqrt(held * group_count - 1)
    x_forward, y_forward, y_back, x_back = tables()
    shape = code_shape(group_count)
    codes = call(
        encode_gradient, "encode_gradient", 1, [gradient], [whole(gradient.shape)],
        whole(shape), jax.ShapeDtypeStruct(shape, jnp.int16), [], 1_000_000,
    )
    levels = lax.all_to_all(codes, "mem", 0, 0, tiled=True)
    offset = (lax.axis_index("grid") * 16).astype(jnp.int32).reshape(1)
    weight = spectral_weight.transpose(0, 2, 1)
    basis_t = eof_basis.T

    def chain(modes):
        message = run_forward(modes, held, 0, mode_count, members, levels, basis_t, x_forward)
        message = lax.all_to_all(message, "grid", 0, 0, tiled=True)
        control, back = run_spectral(
            modes, held, 0, held, member_scale, retained, offset, message, weight, y_back,
            y_forward, None,
        )
        back = lax.all_to_all(back, "grid", 0, 0, tiled=True)
        sums = run_backward(
            modes, group_count, member_scale, mode_count, members, back, eof_basis, x_back
        )
        return sums, control

    most = len(MODE_STEPS) - 1
    branch = sum((mode_count[0] > m).astype(jnp.int32) for m in MODE_STEPS[:most])
    sums, control = lax.switch(branch, [functools.partial(chain, m) for m in MODE_STEPS])
    sums = lax.all_to_all(sums, "mem", 0, 0, tiled=True)
    increment = call(
        add_groups, "add_groups", 1, [sums], [whole(shape)],
        whole(gradient.shape), jax.ShapeDtypeStruct(gradient.shape, F32), [], 1_000_000,
    )
    return (increment, control.transpose(0, 1, 3, 2))


def solution(mesh):
    return jax.shard_map(
        local,
        mesh=mesh,
        in_specs=(
            P("mem", "grid", None),
            P("mem", None, "grid", None),
            P(),
            P(None, None, "grid"),
            P(),
            P(),
        ),
        out_specs=(P("mem", "grid", None), P("mem", None, None, "grid")),
        check_vma=False,
    )
```

```python
import functools
import math

import jax
import jax.numpy as jnp
import numpy as np
from jax import lax
from jax.experimental import pallas as pl
from jax.experimental.pallas import tpu as pltpu
from jax.sharding import PartitionSpec as P

F32 = jnp.float32
BF16 = jnp.bfloat16
LANES = 128
GROUP = 4
MODE_STEPS = (8, 10, 12, 14, 16)
VMEM_LIMIT = 48 * 1024 * 1024


def cosine_table(length, retain_count):
    cells = np.arange(length, dtype=np.float64)
    waves = np.arange(retain_count, dtype=np.float64)
    factor = np.where(waves == 0.0, math.sqrt(1.0 / length), math.sqrt(2.0 / length))
    return np.cos(math.pi * (cells[:, None] + 0.5) * waves[None, :] / length) * factor[None, :]


def table_parts(table):
    high = table.astype(jnp.bfloat16)
    low = (table - high.astype(np.float64)).astype(jnp.bfloat16)
    return high, low


def parts(value):
    high = value.astype(BF16)
    return high, (value - high.astype(F32)).astype(BF16)


def dot(a, b):
    return lax.dot_general(a, b, (((1,), (0,)), ((), ())), preferred_element_type=F32)


def left_parts(value):
    high, low = parts(value)
    return jnp.concatenate([high, low, high], axis=1)


def right_parts(value):
    high, low = parts(value)
    return jnp.concatenate([high, high, low], axis=0)


def regroup(pieces, width):
    pieces = list(pieces)
    count = len(pieces)
    group = lax.broadcasted_iota(jnp.int32, pieces[0].shape, 1) // width
    step = 1
    while step < count:
        upper = (group & step) != 0
        for a in range(count):
            if a & step:
                continue
            low, high = pieces[a], pieces[a | step]
            pieces[a] = jnp.where(upper, pltpu.roll(high, step * width, 1), low)
            pieces[a | step] = jnp.where(
                upper, high, pltpu.roll(low, LANES - step * width, 1)
            )
        step *= 2
    return pieces


def peak(tile):
    return jnp.max(jnp.abs(tile), axis=0, keepdims=True)


def power_of(peaks):
    return jnp.ceil(jnp.log2(jnp.maximum(peaks, 2.0**-80) * (1.0 + 2.0**-12))) - 15.0


def pair_powers(tiles):
    peaks = [peak(t) for t in tiles]
    return power_of(
        jnp.concatenate(
            [functools.reduce(jnp.maximum, peaks[n : n + 2]) for n in range(0, len(peaks), 2)],
            axis=0,
        )
    )


def to_code(scaled):
    return jnp.round(scaled).astype(jnp.int32).astype(jnp.int16)


def from_code(code):
    return code.astype(jnp.int32).astype(F32)


def pick(size, count):
    row = lax.broadcasted_iota(jnp.int32, (size, count), 0) // 16
    return (row == lax.broadcasted_iota(jnp.int32, (size, count), 1)).astype(BF16)


def spread(basis, rows, columns):
    same = (
        lax.broadcasted_iota(jnp.int32, (rows, columns), 0) % 16
        == lax.broadcasted_iota(jnp.int32, (rows, columns), 1) % 16
    )
    out = []
    for part in parts(basis):
        left = dot(pick(rows, 16), part).astype(BF16)
        full = lax.dot_general(
            left, pick(columns, 16), (((1,), (1,)), ((), ())), preferred_element_type=F32
        )
        out.append(jnp.where(same, full, 0.0).astype(BF16))
    return jnp.concatenate([out[0], out[1], out[0]], axis=1)


def masked_basis(basis_ref, mode_count_ref, mode_axis):
    basis = basis_ref[...]
    mode = lax.broadcasted_iota(jnp.int32, basis.shape, mode_axis)
    return jnp.where(mode < mode_count_ref[0], basis, 0.0)


def store_powers(power_ref, message_ref, first_tile):
    groups = power_ref.shape[1]
    for j in range(16):
        for t in range(groups // 4):
            rows = [power_ref[j, 4 * t + g] for g in range(4)]
            message_ref[j, first_tile + t] = to_code(jnp.concatenate(rows, axis=0))


def encode_levels(levels):
    tiles = [
        levels[z][:, q * LANES : (q + 1) * LANES] for z in range(levels.shape[0]) for q in range(4)
    ]
    power = power_of(jnp.concatenate([peak(t) for t in tiles], axis=0))
    shrink = jnp.exp2(-power)
    codes = [to_code(t * shrink[n : n + 1]) for n, t in enumerate(tiles)]
    tail = jnp.concatenate([power, jnp.zeros((16 - len(tiles), LANES), F32)], axis=0)
    return codes + [to_code(tail)]


def decode_levels(code_ref, source):
    tiles = code_ref.shape[1] - 1
    scale = jnp.exp2(from_code(code_ref[source, tiles]))
    values = [from_code(code_ref[source, n]) * scale[n : n + 1] for n in range(tiles)]
    return [jnp.concatenate(values[z : z + 4], axis=1) for z in range(0, tiles, 4)]


def encode_gradient(gradient_ref, code_ref):
    for n, code in enumerate(encode_levels(gradient_ref[...])):
        for target in range(code_ref.shape[0]):
            code_ref[target, n] = code


def add_groups(code_ref, increment_ref):
    total = decode_levels(code_ref, 0)
    for source in range(1, code_ref.shape[0]):
        total = [a + b for a, b in zip(total, decode_levels(code_ref, source))]
    for z, level in enumerate(total):
        increment_ref[z] = level


def forward_rows(
    tiles, modes, mode_count_ref, members_ref, code_ref, basis_ref, table_ref,
    message_ref, spread_ref, power_ref, grad_ref,
):
    step = pl.program_id(0)
    steps = pl.num_programs(0)

    @pl.when(step == 0)
    def _():
        spread_ref[...] = spread(masked_basis(basis_ref, mode_count_ref, 0), modes * 16, 256)
        power_ref[...] = jnp.zeros_like(power_ref)
        share = 16 // code_ref.shape[0]
        for source in range(code_ref.shape[0]):
            for z, level in enumerate(decode_levels(code_ref, source)):
                grad_ref[share * source + z] = level

    product = members_ref[...].astype(F32) * grad_ref[...][None]
    both = left_parts(product.reshape(GROUP * 256, 512))
    spectra = [dot(both[m * 256 : m * 256 + 256], table_ref[...]) for m in range(GROUP)]
    outs = [dot(spread_ref[...], right_parts(spectra[m])) for m in range(GROUP)]
    unit = min(GROUP, 16 // math.gcd(modes, 16))
    for m0 in range(0, GROUP, unit):
        first, count = m0 * modes // 8, unit * modes // 8
        combos = [
            outs[m][k * 16 : k * 16 + 16] for m in range(m0, m0 + unit) for k in range(modes)
        ]
        for jh in range(2):
            pieces = [c[:, jh * LANES : (jh + 1) * LANES] for c in combos]
            powers = [pair_powers(pieces[c::8]) for c in range(8)]
            shrink = [jnp.exp2(-p) for p in powers]
            for t in range(count):
                codes = [to_code(pieces[8 * t + c] * shrink[c][t // 2 : t // 2 + 1]) for c in range(8)]
                for j, code in enumerate(regroup(codes, 16)):
                    message_ref[jh * 8 + j, step * tiles + first + t] = code
            for j, power in enumerate(regroup(powers, 16)):
                power_ref[jh * 8 + j, step, first // 2 : (first + count + 1) // 2, :] = power

    @pl.when(step == steps - 1)
    def _():
        store_powers(power_ref, message_ref, message_ref.shape[1] - power_ref.shape[1] // 4)


def spectral(
    tiles, modes, member_scale, retained_ref, offset_ref, message_ref, weight_ref, back_table_ref,
    table_ref, *rest,
):
    control_ref, back_ref, band_ref, scale_ref, power_ref = rest[-5:]
    step = pl.program_id(0)
    steps = pl.num_programs(0)
    groups = power_ref.shape[1]
    first_tail = message_ref.shape[1] - groups // 4

    @pl.when(step == 0)
    def _():
        for i in range(16):
            for t in range(groups // 4):
                scale = jnp.exp2(from_code(message_ref[i, first_tail + t]))
                for g in range(4):
                    scale_ref[i, 4 * t + g] = scale[4 * g : 4 * g + 4]
        power_ref[...] = jnp.zeros_like(power_ref)
        wave = (
            lax.broadcasted_iota(jnp.int32, (16, LANES), 0)
            + lax.broadcasted_iota(jnp.int32, (16, LANES), 1)
            + offset_ref[0]
        )
        bands = [jnp.where(wave < retained_ref[k], weight_ref[k], 0.0) for k in range(modes)]
        for t in range(tiles):
            tile = jnp.concatenate([bands[(8 * t + c) % modes] for c in range(8)], axis=0)
            band_ref[:, t * LANES : (t + 1) * LANES] = tile.T

    if modes < 16:
        control_ref[:, modes:] = jnp.zeros((GROUP, 16 - modes, 16, LANES), F32)
    lines = []
    for t in range(tiles):
        code = from_code(message_ref[:, step * tiles + t])
        lines.append((code * scale_ref[:, step, t // 2 : t // 2 + 1, :]).reshape(256, LANES))
    band = band_ref[...]
    half = (tiles + 2) // 4 * 2
    spans = ((0, half), (half, tiles))
    controls, backs = [], []
    for t0, t1 in spans:
        control = dot(table_ref[...], right_parts(jnp.concatenate(lines[t0:t1], axis=1)))
        controls.append(control * (band[:, t0 * LANES : t1 * LANES] * member_scale))
    for (t0, t1), control in zip(spans, controls):
        right = right_parts(control * band[:, t0 * LANES : t1 * LANES])
        backs.append(dot(back_table_ref[...], right))
    for (t0, t1), control, back in zip(spans, controls, backs):
        for t in range(t0, t1):
            turned = control[:, (t - t0) * LANES : (t - t0 + 1) * LANES].T
            for c in range(8):
                m, k = divmod(8 * t + c, modes)
                control_ref[m, k] = turned[16 * c : 16 * c + 16]
        for i in range(16):
            rows = back[16 * i : 16 * i + 16]
            pieces = [rows[:, n * LANES : (n + 1) * LANES] for n in range(t1 - t0)]
            power = pair_powers(pieces)
            shrink = jnp.exp2(-power)
            for n, piece in enumerate(pieces):
                scaled = piece * shrink[n // 2 : n // 2 + 1]
                back_ref[i, step * tiles + t0 + n] = to_code(scaled)
            power_ref[i, step, t0 // 2 : (t1 + 1) // 2, :] = power

    @pl.when(step == steps - 1)
    def _():
        store_powers(power_ref, back_ref, first_tail)


def backward_rows(
    tiles, modes, member_scale, mode_count_ref, members_ref, back_ref, basis_ref, table_ref,
    *rest,
):
    code_ref, spread_ref, scale_ref, total_ref = rest
    step = pl.program_id(0)
    groups = scale_ref.shape[2]
    first_tail = back_ref.shape[1] - groups // 4

    @pl.when(step == 0)
    def _():
        basis = masked_basis(basis_ref, mode_count_ref, 1) * member_scale
        spread_ref[...] = spread(basis, 256, modes * 16)
        for jh in range(2):
            for t in range(groups // 4):
                scales = regroup(
                    [jnp.exp2(from_code(back_ref[jh * 8 + j, first_tail + t])) for j in range(8)],
                    16,
                )
                for c in range(8):
                    for g in range(4):
                        scale_ref[jh, c, 4 * t + g] = scales[c][4 * g : 4 * g + 4]
        total_ref[...] = jnp.zeros_like(total_ref)

    halves = []
    for jh in range(2):
        combos = []
        scales = [scale_ref[jh, c, step] for c in range(8)]
        for t in range(tiles):
            codes = [back_ref[jh * 8 + j, step * tiles + t] for j in range(8)]
            for c, code in enumerate(regroup(codes, 16)):
                combos.append(from_code(code) * scales[c][t // 2 : t // 2 + 1])
        halves.append(combos)
    levels = []
    for m in range(GROUP):
        rows = [
            jnp.concatenate(half[m * modes : (m + 1) * modes], axis=0) for half in halves
        ]
        levels.append(dot(spread_ref[...], right_parts(jnp.concatenate(rows, axis=1))))
    vertical = dot(left_parts(jnp.concatenate(levels, axis=0)), table_ref[...])
    values = members_ref[...].astype(F32) * vertical.reshape(GROUP, 16, 16, 512)
    total_ref[...] += jnp.sum(values, axis=0)

    @pl.when(step == pl.num_programs(0) - 1)
    def _():
        share = 16 // code_ref.shape[0]
        for target in range(code_ref.shape[0]):
            levels = total_ref[share * target : share * (target + 1)]
            for n, code in enumerate(encode_levels(levels)):
                code_ref[target, n] = code


def whole(shape):
    return pl.BlockSpec(shape, lambda m: (0,) * len(shape))


SMEM = pl.BlockSpec(memory_space=pltpu.SMEM)


def call(kernel, name, steps, operands, in_specs, out_specs, out_shape, scratch, flops, **more):
    return pl.pallas_call(
        kernel,
        grid=(steps,),
        in_specs=in_specs,
        out_specs=out_specs,
        out_shape=out_shape,
        scratch_shapes=scratch,
        compiler_params=pltpu.CompilerParams(
            dimension_semantics=("arbitrary",), vmem_limit_bytes=VMEM_LIMIT
        ),
        cost_estimate=pl.CostEstimate(
            flops=steps * flops, bytes_accessed=steps * flops // 100, transcendentals=0
        ),
        name=name,
        **more,
    )(*operands)


def stacked(table, axis, order):
    both = table_parts(table)
    return jnp.asarray(np.concatenate([both[i] for i in order], axis=axis))


def tables():
    x_table, y_table = cosine_table(512, 256), cosine_table(256, 128)
    return (
        stacked(x_table, 0, (0, 0, 1)),
        stacked(y_table.T, 1, (0, 1, 0)),
        stacked(y_table, 1, (0, 1, 0)),
        stacked(x_table.T, 0, (0, 0, 1)),
    )


def sizes(modes, count):
    groups = count // GROUP
    tiles = modes * GROUP // 8
    padded = -(-groups // 4) * 4
    shape = (16, groups * tiles + padded // 4, 16, LANES)
    return groups, tiles, padded, jax.ShapeDtypeStruct(shape, jnp.int16)


def member_block(chunk, groups):
    return pl.BlockSpec((GROUP, 16, 16, 512), lambda m: (m + chunk * groups, 0, 0, 0))


def run_forward(modes, count, chunk, mode_count, members, levels, basis_t, table):
    groups, tiles, padded, message = sizes(modes, count)
    return call(
        functools.partial(forward_rows, tiles, modes), "forward_rows", groups,
        (mode_count, members, levels, basis_t, table),
        [SMEM, member_block(chunk, groups)] + [whole(a.shape) for a in (levels, basis_t, table)],
        whole(message.shape), message,
        [
            pltpu.VMEM((modes * 16, 768), BF16),
            pltpu.VMEM((16, padded, 4, LANES), F32),
            pltpu.VMEM((16, 16, 512), F32),
        ],
        1_600_000_000,
    )


def run_spectral(
    modes, count, chunk, held, member_scale, retained, offset, message, weight, back_table, table,
    control,
):
    groups, tiles, padded, kind = sizes(modes, count)
    extra = [] if control is None else [control]
    return call(
        functools.partial(spectral, tiles, modes, member_scale), "spectral", groups,
        [retained, offset, message, weight, back_table, table] + extra,
        [SMEM, SMEM]
        + [whole(a.shape) for a in (message, weight, back_table, table)]
        + [pl.BlockSpec(memory_space=pl.ANY)] * len(extra),
        [
            pl.BlockSpec((GROUP, 16, 16, LANES), lambda m: (m + chunk * groups, 0, 0, 0)),
            whole(kind.shape),
        ],
        [jax.ShapeDtypeStruct((held, 16, 16, LANES), F32), kind],
        [pltpu.VMEM((LANES, tiles * LANES), F32)]
        + [pltpu.VMEM((16, padded, 4, LANES), F32)] * 2,
        1_000_000_000,
        input_output_aliases={6: 0} if extra else {},
    )


def run_backward(modes, group_count, member_scale, mode_count, members, back, basis, table):
    groups, tiles, padded, _ = sizes(modes, members.shape[0])
    shape = code_shape(group_count)
    return call(
        functools.partial(backward_rows, tiles, modes, member_scale), "backward_rows", groups,
        [mode_count, members, back, basis, table],
        [SMEM, member_block(0, groups)] + [whole(a.shape) for a in [back, basis, table]],
        whole(shape), jax.ShapeDtypeStruct(shape, jnp.int16),
        [
            pltpu.VMEM((256, modes * 48), BF16),
            pltpu.VMEM((2, 8, padded, 4, LANES), F32),
            pltpu.VMEM((16, 16, 512), F32),
        ],
        1_600_000_000,
    )


def code_shape(group_count):
    return (group_count, 64 // group_count + 1, 16, LANES)


def local(gradient, members, eof_basis, spectral_weight, retained, mode_count):
    group_count = lax.axis_size("mem")
    held = members.shape[0]
    member_scale = 1.0 / math.sqrt(held * group_count - 1)
    x_forward, y_forward, y_back, x_back = tables()
    shape = code_shape(group_count)
    codes = call(
        encode_gradient, "encode_gradient", 1, [gradient], [whole(gradient.shape)],
        whole(shape), jax.ShapeDtypeStruct(shape, jnp.int16), [], 1_000_000,
    )
    levels = lax.all_to_all(codes, "mem", 0, 0, tiled=True)
    offset = (lax.axis_index("grid") * 16).astype(jnp.int32).reshape(1)
    weight = spectral_weight.transpose(0, 2, 1)
    basis_t = eof_basis.T

    def chain(modes):
        message = run_forward(modes, held, 0, mode_count, members, levels, basis_t, x_forward)
        message = lax.all_to_all(message, "grid", 0, 0, tiled=True)
        control, back = run_spectral(
            modes, held, 0, held, member_scale, retained, offset, message, weight, y_back,
            y_forward, None,
        )
        back = lax.all_to_all(back, "grid", 0, 0, tiled=True)
        sums = run_backward(
            modes, group_count, member_scale, mode_count, members, back, eof_basis, x_back
        )
        return sums, control

    most = len(MODE_STEPS) - 1
    branch = sum((mode_count[0] > m).astype(jnp.int32) for m in MODE_STEPS[:most])
    sums, control = lax.switch(branch, [functools.partial(chain, m) for m in MODE_STEPS])
    sums = lax.all_to_all(sums, "mem", 0, 0, tiled=True)
    increment = call(
        add_groups, "add_groups", 1, [sums], [whole(shape)],
        whole(gradient.shape), jax.ShapeDtypeStruct(gradient.shape, F32), [], 1_000_000,
    )
    return (increment, control.transpose(0, 1, 3, 2))


def solution(mesh):
    return jax.shard_map(
        local,
        mesh=mesh,
        in_specs=(
            P("mem", "grid", None),
            P("mem", None, "grid", None),
            P(),
            P(None, None, "grid"),
            P(),
            P(),
        ),
        out_specs=(P("mem", "grid", None), P("mem", None, None, "grid")),
        check_vma=False,
    )
```

```python
import functools
import math

import jax
import jax.numpy as jnp
import numpy as np
from jax import lax
from jax.experimental import pallas as pl
from jax.experimental.pallas import tpu as pltpu
from jax.sharding import PartitionSpec as P

F32 = jnp.float32
BF16 = jnp.bfloat16
LANES = 128
GROUP = 4
MODE_STEPS = (8, 10, 12, 14, 16)
VMEM_LIMIT = 48 * 1024 * 1024


def cosine_table(length, retain_count):
    cells = np.arange(length, dtype=np.float64)
    waves = np.arange(retain_count, dtype=np.float64)
    factor = np.where(waves == 0.0, math.sqrt(1.0 / length), math.sqrt(2.0 / length))
    return np.cos(math.pi * (cells[:, None] + 0.5) * waves[None, :] / length) * factor[None, :]


def table_parts(table):
    high = table.astype(jnp.bfloat16)
    low = (table - high.astype(np.float64)).astype(jnp.bfloat16)
    return high, low


def parts(value):
    high = value.astype(BF16)
    return high, (value - high.astype(F32)).astype(BF16)


def dot(a, b):
    return lax.dot_general(a, b, (((1,), (0,)), ((), ())), preferred_element_type=F32)


def left_parts(value):
    high, low = parts(value)
    return jnp.concatenate([high, low, high], axis=1)


def right_parts(value):
    high, low = parts(value)
    return jnp.concatenate([high, high, low], axis=0)


def regroup(pieces, width):
    pieces = list(pieces)
    count = len(pieces)
    group = lax.broadcasted_iota(jnp.int32, pieces[0].shape, 1) // width
    step = 1
    while step < count:
        upper = (group & step) != 0
        for a in range(count):
            if a & step:
                continue
            low, high = pieces[a], pieces[a | step]
            pieces[a] = jnp.where(upper, pltpu.roll(high, step * width, 1), low)
            pieces[a | step] = jnp.where(
                upper, high, pltpu.roll(low, LANES - step * width, 1)
            )
        step *= 2
    return pieces


def peak(tile):
    return jnp.max(jnp.abs(tile), axis=0, keepdims=True)


def power_of(peaks):
    return jnp.ceil(jnp.log2(jnp.maximum(peaks, 2.0**-80) * (1.0 + 2.0**-12))) - 15.0


def pair_powers(tiles):
    peaks = [peak(t) for t in tiles]
    return power_of(
        jnp.concatenate(
            [functools.reduce(jnp.maximum, peaks[n : n + 2]) for n in range(0, len(peaks), 2)],
            axis=0,
        )
    )


def to_code(scaled):
    return jnp.round(scaled).astype(jnp.int32).astype(jnp.int16)


def from_code(code):
    return code.astype(jnp.int32).astype(F32)


def pick(size, count):
    row = lax.broadcasted_iota(jnp.int32, (size, count), 0) // 16
    return (row == lax.broadcasted_iota(jnp.int32, (size, count), 1)).astype(BF16)


def spread(basis, rows, columns):
    same = (
        lax.broadcasted_iota(jnp.int32, (rows, columns), 0) % 16
        == lax.broadcasted_iota(jnp.int32, (rows, columns), 1) % 16
    )
    out = []
    for part in parts(basis):
        left = dot(pick(rows, 16), part).astype(BF16)
        full = lax.dot_general(
            left, pick(columns, 16), (((1,), (1,)), ((), ())), preferred_element_type=F32
        )
        out.append(jnp.where(same, full, 0.0).astype(BF16))
    return jnp.concatenate([out[0], out[1], out[0]], axis=1)


def masked_basis(basis_ref, mode_count_ref, mode_axis):
    basis = basis_ref[...]
    mode = lax.broadcasted_iota(jnp.int32, basis.shape, mode_axis)
    return jnp.where(mode < mode_count_ref[0], basis, 0.0)


def store_powers(power_ref, message_ref, first_tile):
    groups = power_ref.shape[1]
    for j in range(16):
        for t in range(groups // 4):
            rows = [power_ref[j, 4 * t + g] for g in range(4)]
            message_ref[j, first_tile + t] = to_code(jnp.concatenate(rows, axis=0))


def encode_levels(levels):
    tiles = [
        levels[z][:, q * LANES : (q + 1) * LANES] for z in range(levels.shape[0]) for q in range(4)
    ]
    power = power_of(jnp.concatenate([peak(t) for t in tiles], axis=0))
    shrink = jnp.exp2(-power)
    codes = [to_code(t * shrink[n : n + 1]) for n, t in enumerate(tiles)]
    tail = jnp.concatenate([power, jnp.zeros((16 - len(tiles), LANES), F32)], axis=0)
    return codes + [to_code(tail)]


def decode_levels(code_ref, source):
    tiles = code_ref.shape[1] - 1
    scale = jnp.exp2(from_code(code_ref[source, tiles]))
    values = [from_code(code_ref[source, n]) * scale[n : n + 1] for n in range(tiles)]
    return [jnp.concatenate(values[z : z + 4], axis=1) for z in range(0, tiles, 4)]


def encode_gradient(gradient_ref, code_ref):
    for n, code in enumerate(encode_levels(gradient_ref[...])):
        for target in range(code_ref.shape[0]):
            code_ref[target, n] = code


def add_groups(code_ref, increment_ref):
    total = decode_levels(code_ref, 0)
    for source in range(1, code_ref.shape[0]):
        total = [a + b for a, b in zip(total, decode_levels(code_ref, source))]
    for z, level in enumerate(total):
        increment_ref[z] = level


def forward_unit(modes):
    return {8: 2, 12: 2, 16: 1}.get(modes, GROUP)


def forward_row(modes, tile):
    count = forward_unit(modes) * modes // 8
    return tile // count * ((count + 1) // 2) + tile % count // 2


def forward_rows(
    tiles, modes, mode_count_ref, members_ref, code_ref, basis_ref, table_ref,
    message_ref, spread_ref, power_ref, grad_ref,
):
    step = pl.program_id(0)
    steps = pl.num_programs(0)

    @pl.when(step == 0)
    def _():
        spread_ref[...] = spread(masked_basis(basis_ref, mode_count_ref, 0), modes * 16, 256)
        power_ref[...] = jnp.zeros_like(power_ref)
        share = 16 // code_ref.shape[0]
        for source in range(code_ref.shape[0]):
            for z, level in enumerate(decode_levels(code_ref, source)):
                grad_ref[share * source + z] = level

    product = members_ref[...].astype(F32) * grad_ref[...][None]
    both = left_parts(product.reshape(GROUP * 256, 512))
    spectra = [dot(both[m * 256 : m * 256 + 256], table_ref[...]) for m in range(GROUP)]
    rights = [right_parts(spectrum) for spectrum in spectra]
    cut = modes * 8 if modes == 16 else modes * 16
    outs = [
        jnp.concatenate([dot(spread_ref[r : r + cut], right) for r in range(0, modes * 16, cut)])
        for right in rights
    ]
    unit = forward_unit(modes)
    for m0 in range(0, GROUP, unit):
        first, count = m0 * modes // 8, unit * modes // 8
        combos = [
            outs[m][k * 16 : k * 16 + 16] for m in range(m0, m0 + unit) for k in range(modes)
        ]
        for jh in range(2):
            pieces = [c[:, jh * LANES : (jh + 1) * LANES] for c in combos]
            powers = [pair_powers(pieces[c::8]) for c in range(8)]
            shrink = [jnp.exp2(-p) for p in powers]
            for t in range(count):
                codes = [to_code(pieces[8 * t + c] * shrink[c][t // 2 : t // 2 + 1]) for c in range(8)]
                for j, code in enumerate(regroup(codes, 16)):
                    message_ref[jh * 8 + j, step * tiles + first + t] = code
            for j, power in enumerate(regroup(powers, 16)):
                row = forward_row(modes, first)
                power_ref[jh * 8 + j, step, row : row + (count + 1) // 2, :] = power

    @pl.when(step == steps - 1)
    def _():
        store_powers(power_ref, message_ref, message_ref.shape[1] - power_ref.shape[1] // 4)


def spectral(
    tiles, modes, member_scale, retained_ref, offset_ref, message_ref, weight_ref, back_table_ref,
    table_ref, *rest,
):
    control_ref, back_ref, band_ref, scale_ref, power_ref = rest[-5:]
    step = pl.program_id(0)
    steps = pl.num_programs(0)
    groups = power_ref.shape[1]
    first_tail = message_ref.shape[1] - groups // 4

    @pl.when(step == 0)
    def _():
        for i in range(16):
            for t in range(groups // 4):
                scale = jnp.exp2(from_code(message_ref[i, first_tail + t]))
                for g in range(4):
                    scale_ref[i, 4 * t + g] = scale[4 * g : 4 * g + 4]
        power_ref[...] = jnp.zeros_like(power_ref)
        wave = (
            lax.broadcasted_iota(jnp.int32, (16, LANES), 0)
            + lax.broadcasted_iota(jnp.int32, (16, LANES), 1)
            + offset_ref[0]
        )
        bands = [jnp.where(wave < retained_ref[k], weight_ref[k], 0.0) for k in range(modes)]
        for t in range(tiles):
            tile = jnp.concatenate([bands[(8 * t + c) % modes] for c in range(8)], axis=0)
            band_ref[:, t * LANES : (t + 1) * LANES] = tile.T

    if modes < 16:
        control_ref[:, modes:] = jnp.zeros((GROUP, 16 - modes, 16, LANES), F32)
    lines = []
    for t in range(tiles):
        code, row = from_code(message_ref[:, step * tiles + t]), forward_row(modes, t)
        lines.append((code * scale_ref[:, step, row : row + 1, :]).reshape(256, LANES))
    band = band_ref[...]
    half = (tiles + 2) // 4 * 2
    spans = ((0, half), (half, tiles))
    controls, backs = [], []
    for t0, t1 in spans:
        control = dot(table_ref[...], right_parts(jnp.concatenate(lines[t0:t1], axis=1)))
        controls.append(control * (band[:, t0 * LANES : t1 * LANES] * member_scale))
    for (t0, t1), control in zip(spans, controls):
        right = right_parts(control * band[:, t0 * LANES : t1 * LANES])
        backs.append(dot(back_table_ref[...], right))
    for (t0, t1), control, back in zip(spans, controls, backs):
        for t in range(t0, t1):
            turned = control[:, (t - t0) * LANES : (t - t0 + 1) * LANES].T
            for c in range(8):
                m, k = divmod(8 * t + c, modes)
                control_ref[m, k] = turned[16 * c : 16 * c + 16]
        for i in range(16):
            rows = back[16 * i : 16 * i + 16]
            pieces = [rows[:, n * LANES : (n + 1) * LANES] for n in range(t1 - t0)]
            power = pair_powers(pieces)
            shrink = jnp.exp2(-power)
            for n, piece in enumerate(pieces):
                scaled = piece * shrink[n // 2 : n // 2 + 1]
                back_ref[i, step * tiles + t0 + n] = to_code(scaled)
            power_ref[i, step, t0 // 2 : (t1 + 1) // 2, :] = power

    @pl.when(step == steps - 1)
    def _():
        store_powers(power_ref, back_ref, first_tail)


def backward_rows(
    tiles, modes, member_scale, mode_count_ref, members_ref, back_ref, basis_ref, table_ref,
    *rest,
):
    code_ref, spread_ref, scale_ref, total_ref = rest
    step = pl.program_id(0)
    groups = scale_ref.shape[2]
    first_tail = back_ref.shape[1] - groups // 4

    @pl.when(step == 0)
    def _():
        basis = masked_basis(basis_ref, mode_count_ref, 1) * member_scale
        spread_ref[...] = spread(basis, 256, modes * 16)
        for jh in range(2):
            for t in range(groups // 4):
                scales = regroup(
                    [jnp.exp2(from_code(back_ref[jh * 8 + j, first_tail + t])) for j in range(8)],
                    16,
                )
                for c in range(8):
                    for g in range(4):
                        scale_ref[jh, c, 4 * t + g] = scales[c][4 * g : 4 * g + 4]
        total_ref[...] = jnp.zeros_like(total_ref)

    halves = []
    for jh in range(2):
        combos = []
        scales = [scale_ref[jh, c, step] for c in range(8)]
        for t in range(tiles):
            codes = [back_ref[jh * 8 + j, step * tiles + t] for j in range(8)]
            for c, code in enumerate(regroup(codes, 16)):
                combos.append(from_code(code) * scales[c][t // 2 : t // 2 + 1])
        halves.append(combos)
    levels = []
    for m in range(GROUP):
        rows = [
            jnp.concatenate(half[m * modes : (m + 1) * modes], axis=0) for half in halves
        ]
        levels.append(dot(spread_ref[...], right_parts(jnp.concatenate(rows, axis=1))))
    vertical = dot(left_parts(jnp.concatenate(levels, axis=0)), table_ref[...])
    values = members_ref[...].astype(F32) * vertical.reshape(GROUP, 16, 16, 512)
    total_ref[...] += jnp.sum(values, axis=0)

    @pl.when(step == pl.num_programs(0) - 1)
    def _():
        share = 16 // code_ref.shape[0]
        for target in range(code_ref.shape[0]):
            levels = total_ref[share * target : share * (target + 1)]
            for n, code in enumerate(encode_levels(levels)):
                code_ref[target, n] = code


def whole(shape):
    return pl.BlockSpec(shape, lambda m: (0,) * len(shape))


SMEM = pl.BlockSpec(memory_space=pltpu.SMEM)


def call(kernel, name, steps, operands, in_specs, out_specs, out_shape, scratch, flops, **more):
    return pl.pallas_call(
        kernel,
        grid=(steps,),
        in_specs=in_specs,
        out_specs=out_specs,
        out_shape=out_shape,
        scratch_shapes=scratch,
        compiler_params=pltpu.CompilerParams(
            dimension_semantics=("arbitrary",), vmem_limit_bytes=VMEM_LIMIT
        ),
        cost_estimate=pl.CostEstimate(
            flops=steps * flops, bytes_accessed=steps * flops // 100, transcendentals=0
        ),
        name=name,
        **more,
    )(*operands)


def stacked(table, axis, order):
    both = table_parts(table)
    return jnp.asarray(np.concatenate([both[i] for i in order], axis=axis))


def tables():
    x_table, y_table = cosine_table(512, 256), cosine_table(256, 128)
    return (
        stacked(x_table, 0, (0, 0, 1)),
        stacked(y_table.T, 1, (0, 1, 0)),
        stacked(y_table, 1, (0, 1, 0)),
        stacked(x_table.T, 0, (0, 0, 1)),
    )


def sizes(modes, count):
    groups = count // GROUP
    tiles = modes * GROUP // 8
    padded = -(-groups // 4) * 4
    shape = (16, groups * tiles + padded // 4, 16, LANES)
    return groups, tiles, padded, jax.ShapeDtypeStruct(shape, jnp.int16)


def member_block(chunk, groups):
    return pl.BlockSpec((GROUP, 16, 16, 512), lambda m: (m + chunk * groups, 0, 0, 0))


def run_forward(modes, count, chunk, mode_count, members, levels, basis_t, table):
    groups, tiles, padded, message = sizes(modes, count)
    return call(
        functools.partial(forward_rows, tiles, modes), "forward_rows", groups,
        (mode_count, members, levels, basis_t, table),
        [SMEM, member_block(chunk, groups)] + [whole(a.shape) for a in (levels, basis_t, table)],
        whole(message.shape), message,
        [
            pltpu.VMEM((modes * 16, 768), BF16),
            pltpu.VMEM((16, padded, 4, LANES), F32),
            pltpu.VMEM((16, 16, 512), F32),
        ],
        1_600_000_000,
    )


def run_spectral(
    modes, count, chunk, held, member_scale, retained, offset, message, weight, back_table, table,
    control,
):
    groups, tiles, padded, kind = sizes(modes, count)
    extra = [] if control is None else [control]
    return call(
        functools.partial(spectral, tiles, modes, member_scale), "spectral", groups,
        [retained, offset, message, weight, back_table, table] + extra,
        [SMEM, SMEM]
        + [whole(a.shape) for a in (message, weight, back_table, table)]
        + [pl.BlockSpec(memory_space=pl.ANY)] * len(extra),
        [
            pl.BlockSpec((GROUP, 16, 16, LANES), lambda m: (m + chunk * groups, 0, 0, 0)),
            whole(kind.shape),
        ],
        [jax.ShapeDtypeStruct((held, 16, 16, LANES), F32), kind],
        [pltpu.VMEM((LANES, tiles * LANES), F32)]
        + [pltpu.VMEM((16, padded, 4, LANES), F32)] * 2,
        1_000_000_000,
        input_output_aliases={6: 0} if extra else {},
    )


def run_backward(modes, group_count, member_scale, mode_count, members, back, basis, table):
    groups, tiles, padded, _ = sizes(modes, members.shape[0])
    shape = code_shape(group_count)
    return call(
        functools.partial(backward_rows, tiles, modes, member_scale), "backward_rows", groups,
        [mode_count, members, back, basis, table],
        [SMEM, member_block(0, groups)] + [whole(a.shape) for a in [back, basis, table]],
        whole(shape), jax.ShapeDtypeStruct(shape, jnp.int16),
        [
            pltpu.VMEM((256, modes * 48), BF16),
            pltpu.VMEM((2, 8, padded, 4, LANES), F32),
            pltpu.VMEM((16, 16, 512), F32),
        ],
        1_600_000_000,
    )


def code_shape(group_count):
    return (group_count, 64 // group_count + 1, 16, LANES)


def local(gradient, members, eof_basis, spectral_weight, retained, mode_count):
    group_count = lax.axis_size("mem")
    held = members.shape[0]
    member_scale = 1.0 / math.sqrt(held * group_count - 1)
    x_forward, y_forward, y_back, x_back = tables()
    shape = code_shape(group_count)
    codes = call(
        encode_gradient, "encode_gradient", 1, [gradient], [whole(gradient.shape)],
        whole(shape), jax.ShapeDtypeStruct(shape, jnp.int16), [], 1_000_000,
    )
    levels = lax.all_to_all(codes, "mem", 0, 0, tiled=True)
    offset = (lax.axis_index("grid") * 16).astype(jnp.int32).reshape(1)
    weight = spectral_weight.transpose(0, 2, 1)
    basis_t = eof_basis.T

    def chain(modes):
        message = run_forward(modes, held, 0, mode_count, members, levels, basis_t, x_forward)
        message = lax.all_to_all(message, "grid", 0, 0, tiled=True)
        control, back = run_spectral(
            modes, held, 0, held, member_scale, retained, offset, message, weight, y_back,
            y_forward, None,
        )
        back = lax.all_to_all(back, "grid", 0, 0, tiled=True)
        sums = run_backward(
            modes, group_count, member_scale, mode_count, members, back, eof_basis, x_back
        )
        return sums, control

    most = len(MODE_STEPS) - 1
    branch = sum((mode_count[0] > m).astype(jnp.int32) for m in MODE_STEPS[:most])
    sums, control = lax.switch(branch, [functools.partial(chain, m) for m in MODE_STEPS])
    sums = lax.all_to_all(sums, "mem", 0, 0, tiled=True)
    increment = call(
        add_groups, "add_groups", 1, [sums], [whole(shape)],
        whole(gradient.shape), jax.ShapeDtypeStruct(gradient.shape, F32), [], 1_000_000,
    )
    return (increment, control.transpose(0, 1, 3, 2))


def solution(mesh):
    return jax.shard_map(
        local,
        mesh=mesh,
        in_specs=(
            P("mem", "grid", None),
            P("mem", None, "grid", None),
            P(),
            P(None, None, "grid"),
            P(),
            P(),
        ),
        out_specs=(P("mem", "grid", None), P("mem", None, None, "grid")),
        check_vma=False,
    )
```
